32 devices in a mesh: wide: 8 (over z, y), narrow: 4 (over x, core).
Axes of the slice: x: 2, y: 2, z: 4, core: 2. Of those that a mesh axis runs over, the one named last changes fastest.
Arguments:
- buoy_coef: bfloat16 [4, 512, 1024], P(None, 'narrow', 'wide'), may hold values from -300 to 300, as said below
- velocity: bfloat16 [3, 4, 768, 1536], P(None, 'narrow', 'wide'), may hold values from -6 to 6
- buoy_dy: bfloat16 [4, 768, 1536], P('narrow', 'wide'), may hold values from -6 to 6
Outputs:
- advect: bfloat16 [4, 512, 1024], P(None, 'narrow', 'wide')
- buoy_grid: bfloat16 [4, 768, 1536], P('narrow', 'wide')
The draws below stay inside these ranges and needn't reach their ends.
Inputs may be any that keep to these rules, and one draw needn't show every extreme that they name: `buoy_coef`: spectral coefficients of the buoyancy.
All inputs are finite; a program needn't handle non-finite values.
Results may differ from the reference program's by a relative error of at most 0.0087.
Values may be sent and summed in bfloat16 or wider, within the bound.
A program may use at most 64 MiB of HBM per device.

```python
import math
import jax
import jax.numpy as jnp
from jax import lax

KX = 1024
KZ = 512
YS = 4
GX = 1536
GZ = 768


def draw_buoy_coef(key, part):
    noise_key = jax.random.fold_in(jax.random.fold_in(key, 11), 0)
    shape_full = (YS, KZ, KX)
    noises = jax.random.truncated_normal(noise_key, -6.0, 6.0, shape_full, jnp.float32)
    x_mode = (lax.iota(jnp.int32, KX) // 2).astype(jnp.float32)
    z_degree = lax.iota(jnp.int32, KZ).astype(jnp.float32)
    x_shape = 1.0 / jnp.sqrt(1.0 + x_mode / 64.0)
    z_shape = 1.0 / (1.0 + z_degree / 8.0)
    return (50.0 * noises * z_shape[None, :, None] * x_shape[None, None, :]).astype(jnp.bfloat16)


def block_levels(key, shape, shards, least, largest):
    factor_of = 1.0
    for position, parts in shards:
        heights = jax.random.uniform(jax.random.fold_in(jax.random.fold_in(key, 6), position), (parts,), jnp.float32, least / len(shards), largest / len(shards))
        factor_of = factor_of * jnp.repeat(jnp.exp(heights), shape[position] // parts).reshape((-1,) + (1,) * (len(shape) - 1 - position))
    return factor_of


def bell_draw(stream_key, shape, width, most, cuts=(), kind=jnp.bfloat16):
    drawn = width * jax.random.normal(stream_key, shape, jnp.float32)
    if cuts:
        drawn = drawn * block_levels(stream_key, shape, cuts, -0.22, 0.18)
    return jnp.clip(drawn, -most, most).astype(kind)


def setup_inputs(seed: int = 0) -> dict:
    keys = jax.random.split(jax.random.key(seed), 4)
    return {
        "buoy_coef": draw_buoy_coef(jax.random.fold_in(keys[3], 71), 0),
        "velocity": bell_draw(keys[1], (3, YS, GZ, GX), 1.0, 6.0, ((1, 4), (2, 8))),
        "buoy_dy": bell_draw(keys[2], (YS, GZ, GX), 1.0, 6.0, ((0, 4), (1, 8))),
    }


def x_table(offset, width_now, kx_size, gx_size):
    points = offset + lax.iota(jnp.int32, width_now)[:, None]
    column_id = lax.iota(jnp.int32, kx_size)[None, :]
    harmonic = column_id // 2
    phase_id = harmonic * points % gx_size
    angles = phase_id.astype(jnp.float32) * (2.0 * math.pi / gx_size)
    weights = jnp.where(harmonic == 0, math.sqrt(1.0 / gx_size), math.sqrt(2.0 / gx_size)).astype(jnp.float32)
    basis_raw = jnp.where(column_id % 2 == 0, jnp.cos(angles), jnp.sin(angles))
    return (basis_raw * weights).astype(jnp.bfloat16)

def z_tables(gz_size, kz_size):
    nodes = lax.iota(jnp.int32, gz_size)[:, None]
    degree = lax.iota(jnp.int32, kz_size)[None, :]
    phase_id = degree * (2 * nodes + 1) % (4 * gz_size)
    angles = phase_id.astype(jnp.float32) * (math.pi / (2.0 * gz_size))
    polar = (2 * nodes + 1).astype(jnp.float32) * (math.pi / (2.0 * gz_size))
    weights = jnp.where(degree == 0, math.sqrt(1.0 / gz_size), math.sqrt(2.0 / gz_size)).astype(jnp.float32)
    values = (weights * jnp.cos(angles)).astype(jnp.bfloat16)
    slopes = (weights * (2.0 / gz_size) * degree.astype(jnp.float32) * jnp.sin(angles) / jnp.sin(polar)).astype(jnp.bfloat16)
    return (values, slopes)

def x_slope(wave_in, offset, gx_size):
    width_now = wave_in.shape[-1]
    paired = wave_in.astype(jnp.float32).reshape(wave_in.shape[:-1] + (width_now // 2, 2))
    harmonic = (offset // 2 + lax.iota(jnp.int32, width_now // 2)).astype(jnp.float32)
    omega_rate = harmonic * (2.0 * math.pi / gx_size)
    cos_part = omega_rate * paired[..., 1]
    sin_part = -omega_rate * paired[..., 0]
    return jnp.stack([cos_part, sin_part], axis=-1).reshape(wave_in.shape).astype(jnp.bfloat16)

def reference(buoy_coef, velocity, buoy_dy):
    highest = lax.Precision.HIGHEST
    values, slopes = z_tables(GZ, KZ)
    values_wide = values.astype(jnp.float32)
    slopes_wide = slopes.astype(jnp.float32)
    basis_wide = x_table(0, GX, KX, GX).astype(jnp.float32)

    def one_plane(inputs):
        coefs_plane, speed_plane, slope_plane = inputs
        coefs_wide = coefs_plane.astype(jnp.float32)
        wave_val = jnp.dot(values_wide, coefs_wide, precision=highest).astype(jnp.bfloat16)
        wave_dz = jnp.dot(slopes_wide, coefs_wide, precision=highest).astype(jnp.bfloat16)
        wave_dx = x_slope(wave_val, 0, GX)
        grid_val = jnp.dot(wave_val.astype(jnp.float32), basis_wide.T, precision=highest)
        grid_dx = jnp.dot(wave_dx.astype(jnp.float32), basis_wide.T, precision=highest)
        grid_dz = jnp.dot(wave_dz.astype(jnp.float32), basis_wide.T, precision=highest)
        speeds = speed_plane.astype(jnp.float32)
        advect_grid = (-(speeds[0] * grid_dx + speeds[1] * slope_plane.astype(jnp.float32) + speeds[2] * grid_dz)).astype(jnp.bfloat16)
        half_coef = jnp.dot(advect_grid.astype(jnp.float32), basis_wide, precision=highest).astype(jnp.bfloat16)
        result = jnp.dot(values_wide.T, half_coef.astype(jnp.float32), precision=highest).astype(jnp.bfloat16)
        return (result, grid_val.astype(jnp.bfloat16))
    advect, buoy_grid = lax.map(one_plane, (buoy_coef, jnp.moveaxis(velocity, 1, 0), buoy_dy))
    return (advect, buoy_grid)
```

```python
import functools
import math

import jax
import jax.numpy as jnp
import ml_dtypes
import numpy as np
from jax import lax
from jax.experimental import pallas as pl
from jax.experimental.pallas import tpu as pltpu
from jax.sharding import PartitionSpec as P

MESH = pl.DeviceIdType.MESH
F32 = jnp.float32
BF16 = jnp.bfloat16
LANES = 128


def x_table(gx_size, kx_size):
    points = np.arange(gx_size, dtype=np.int32)[:, None]
    column_id = np.arange(kx_size, dtype=np.int32)[None, :]
    harmonic = column_id // 2
    angles = (harmonic * points % gx_size).astype(np.float32) * np.float32(2.0 * math.pi / gx_size)
    weights = np.where(
        harmonic == 0, math.sqrt(1.0 / gx_size), math.sqrt(2.0 / gx_size)
    ).astype(np.float32)
    raw = np.where(column_id % 2 == 0, np.cos(angles), np.sin(angles))
    return (raw * weights).astype(ml_dtypes.bfloat16)


def z_tables(gz_size, kz_size):
    nodes = np.arange(gz_size, dtype=np.int32)[:, None]
    degree = np.arange(kz_size, dtype=np.int32)[None, :]
    step = np.float32(math.pi / (2.0 * gz_size))
    angles = (degree * (2 * nodes + 1) % (4 * gz_size)).astype(np.float32) * step
    polar = (2 * nodes + 1).astype(np.float32) * step
    weights = np.where(
        degree == 0, math.sqrt(1.0 / gz_size), math.sqrt(2.0 / gz_size)
    ).astype(np.float32)
    values = weights * np.cos(angles)
    slopes = weights * np.float32(2.0 / gz_size) * degree.astype(np.float32)
    slopes = slopes * np.sin(angles) / np.sin(polar)
    return values.astype(ml_dtypes.bfloat16), slopes.astype(ml_dtypes.bfloat16)


def dot(left, right):
    return jnp.dot(left, right, preferred_element_type=F32)


def flip_bits(index, mask, size):
    total, bit = 0, 1
    while bit < size:
        digit = lax.rem(lax.div(index, bit), 2)
        total = total + bit * (1 - digit if mask & bit else digit)
        bit *= 2
    return total


def kernel(
    wide, narrow, rows, gx_size,
    coef, velocity, slope_y, zt_hbm, bt_hbm, b_hbm, vt_hbm,
    advect_out, grid_out,
    zt, bt, b, vt, speed, dy,
    recv_a, send_b, recv_b, acc, adv, buoy, send_e, recv_e, send_f,
    local_sem, a_send, a_recv, b_send, b_recv, e_send, e_recv, f_send, f_recv,
):
    pairs = wide // 2
    w = lax.axis_index("wide")
    m = lax.axis_index("narrow")
    mine = lax.div(w, 2)
    beside = 2 * mine + 1 - lax.rem(w, 2)
    narrow_peers = [lax.rem(m + r, narrow) for r in range(1, narrow)]
    pair_of = [flip_bits(mine, t, pairs) for t in range(pairs)]
    far_first = list(range(pairs - 1, 0, -1))

    own = pltpu.make_async_copy(coef.at[m], recv_a.at[m], local_sem.at[0])
    own.start()
    loads = [
        pltpu.make_async_copy(src, dst, local_sem.at[1 + i])
        for i, (src, dst) in enumerate(
            [(zt_hbm, zt), (bt_hbm, bt), (velocity, speed), (slope_y, dy), (b_hbm, b), (vt_hbm, vt)]
        )
    ]
    for load in loads:
        load.start()

    barrier = pltpu.get_barrier_semaphore()
    for peer in narrow_peers:
        pl.semaphore_signal(barrier, inc=1, device_id={"narrow": peer}, device_id_type=MESH)
    for t in range(1, wide):
        pl.semaphore_signal(
            barrier, inc=1, device_id={"wide": lax.rem(w + t, wide)}, device_id_type=MESH
        )
    pl.semaphore_wait(barrier, narrow + wide - 2)

    sends = []

    def push(src, dst, send_sem, recv_sem, target):
        copy = pltpu.make_async_remote_copy(
            src_ref=src, dst_ref=dst, send_sem=send_sem, recv_sem=recv_sem,
            device_id=target, device_id_type=MESH,
        )
        copy.start()
        sends.append(copy)

    def arrived(dst, recv_sem, send_sem, target):
        pltpu.make_async_remote_copy(
            src_ref=dst, dst_ref=dst, send_sem=send_sem, recv_sem=recv_sem,
            device_id=target, device_id_type=MESH,
        ).wait_recv()

    for peer in narrow_peers:
        push(coef.at[peer], recv_a.at[m], a_send.at[peer], a_recv.at[m], {"narrow": peer})
    own.wait()
    loads[0].wait()
    for peer in narrow_peers:
        arrived(recv_a.at[peer], a_recv.at[peer], a_send.at[peer], {"narrow": peer})

    plane = recv_a[...].reshape(-1, LANES)

    def send_points(d):
        send_b[d] = dot(zt[d], plane).astype(BF16)
        push(send_b.at[d], recv_b.at[w], b_send.at[d], b_recv.at[w], {"wide": d})

    for t in far_first:
        send_points(2 * pair_of[t])
        send_points(2 * pair_of[t] + 1)
    send_points(beside)
    recv_b[w] = dot(zt[w], plane).astype(BF16)

    lane = lax.broadcasted_iota(jnp.int32, (1, LANES), 1)
    even = lax.rem(lane, 2) == 0

    def slope_of(field, first):
        harmonic = (lax.div(lane, 2) + first).astype(F32)
        rate = harmonic * (2.0 * math.pi / gx_size)
        wide_field = field.astype(F32)
        after = pltpu.roll(wide_field, LANES - 1, 1)
        before = pltpu.roll(wide_field, 1, 1)
        return jnp.where(even, rate * after, -rate * before).astype(BF16)

    def stacked(pair):
        fields = []
        for s in (0, 1):
            block = recv_b[2 * pair + s]
            val, dz = block[:rows], block[rows:]
            dx = slope_of(val, (2 * pair + s) * (LANES // 2))
            fields.append(jnp.concatenate([val, dx, dz], axis=0))
        return jnp.concatenate(fields, axis=1)

    tile = 512
    cuts = [slice(c, c + tile) for c in range(0, gx_size, tile)]
    for t in range(pairs):
        pair = pair_of[t]
        if t == 0:
            arrived(recv_b.at[beside], b_recv.at[beside], b_send.at[beside], {"wide": beside})
            loads[1].wait()
        else:
            for d in (2 * pair, 2 * pair + 1):
                arrived(recv_b.at[d], b_recv.at[d], b_send.at[d], {"wide": d})
        fields = stacked(pair)
        if t == pairs - 1:
            loads[2].wait()
            loads[3].wait()
        for cut in cuts:
            part = dot(fields, bt[pair, :, cut])
            if t > 0:
                part = part + acc[:, cut]
            if t < pairs - 1:
                acc[:, cut] = part
            else:
                buoy[0, :, cut] = part[:rows].astype(BF16)
                total = speed[0, 0, :, cut].astype(F32) * part[rows : 2 * rows]
                total = total + speed[1, 0, :, cut].astype(F32) * dy[0, :, cut].astype(F32)
                total = total + speed[2, 0, :, cut].astype(F32) * part[2 * rows :]
                adv[:, cut] = (-total).astype(BF16)
    grid_copy = pltpu.make_async_copy(buoy, grid_out, local_sem.at[7])
    grid_copy.start()

    loads[4].wait()
    for t in far_first + [0]:
        pair = pair_of[t]
        half = dot(adv[...], b[pair]).astype(BF16)
        for s in (0, 1):
            send_e[2 * pair + s] = half[:, s * LANES : (s + 1) * LANES]
        for d in (2 * pair, 2 * pair + 1) if t else (beside,):
            push(send_e.at[d], recv_e.at[w], e_send.at[d], e_recv.at[w], {"wide": d})
    recv_e[w] = send_e[w]
    loads[5].wait()
    for t in range(pairs):
        for d in (2 * pair_of[t], 2 * pair_of[t] + 1) if t else (beside,):
            arrived(recv_e.at[d], e_recv.at[d], e_send.at[d], {"wide": d})

    points = recv_e[...].reshape(-1, LANES)
    for peer in narrow_peers:
        send_f[peer] = dot(vt[peer], points).astype(BF16)
        push(send_f.at[peer], advect_out.at[m], f_send.at[peer], f_recv.at[m], {"narrow": peer})
    advect_out[m] = dot(vt[m], points).astype(BF16)
    for peer in narrow_peers:
        arrived(advect_out.at[peer], f_recv.at[peer], f_send.at[peer], {"narrow": peer})
    grid_copy.wait()
    for copy in sends:
        copy.wait_send()


def by_kernel(wide, narrow, coef, velocity, slope_y):
    degrees = coef.shape[1]
    rows, gx_size = slope_y.shape[1:]
    kz_size, kx_size, gz_size = degrees * narrow, LANES * wide, rows * wide
    pairs = wide // 2
    values, slopes = z_tables(gz_size, kz_size)
    basis = x_table(gx_size, kx_size)
    zt = np.concatenate(
        [values.reshape(wide, rows, kz_size), slopes.reshape(wide, rows, kz_size)], axis=1
    )
    bt = np.ascontiguousarray(basis.T).reshape(pairs, 2 * LANES, gx_size)
    b = np.ascontiguousarray(basis.reshape(gx_size, pairs, 2 * LANES).transpose(1, 0, 2))
    vt = np.ascontiguousarray(values.T).reshape(narrow, degrees, gz_size)
    hbm = pl.BlockSpec(memory_space=pltpu.HBM)
    dma = pltpu.SemaphoreType.DMA
    return pl.pallas_call(
        functools.partial(kernel, wide, narrow, rows, gx_size),
        out_shape=(
            jax.ShapeDtypeStruct(coef.shape, BF16),
            jax.ShapeDtypeStruct(slope_y.shape, BF16),
        ),
        in_specs=[hbm] * 7,
        out_specs=(pl.BlockSpec(memory_space=pltpu.VMEM), hbm),
        scratch_shapes=[
            pltpu.VMEM(zt.shape, BF16),
            pltpu.VMEM(bt.shape, BF16),
            pltpu.VMEM(b.shape, BF16),
            pltpu.VMEM(vt.shape, BF16),
            pltpu.VMEM(velocity.shape, BF16),
            pltpu.VMEM(slope_y.shape, BF16),
            pltpu.VMEM((narrow, degrees, LANES), BF16),
            pltpu.VMEM((wide, 2 * rows, LANES), BF16),
            pltpu.VMEM((wide, 2 * rows, LANES), BF16),
            pltpu.VMEM((3 * rows, gx_size), F32),
            pltpu.VMEM((rows, gx_size), BF16),
            pltpu.VMEM(slope_y.shape, BF16),
            pltpu.VMEM((wide, rows, LANES), BF16),
            pltpu.VMEM((wide, rows, LANES), BF16),
            pltpu.VMEM((narrow, degrees, LANES), BF16),
            dma((8,)),
            dma((narrow,)),
            dma((narrow,)),
            dma((wide,)),
            dma((wide,)),
            dma((wide,)),
            dma((wide,)),
            dma((narrow,)),
            dma((narrow,)),
        ],
        compiler_params=pltpu.CompilerParams(
            collective_id=0, has_side_effects=True, vmem_limit_bytes=40 * 1024 * 1024
        ),
    )(coef, velocity, slope_y, zt, bt, b, vt)


def x_slope(wave_in, gx_size):
    width_now = wave_in.shape[-1]
    paired = wave_in.astype(F32).reshape(wave_in.shape[:-1] + (width_now // 2, 2))
    harmonic = lax.iota(jnp.int32, width_now // 2).astype(F32)
    omega_rate = harmonic * (2.0 * math.pi / gx_size)
    cos_part = omega_rate * paired[..., 1]
    sin_part = -omega_rate * paired[..., 0]
    return jnp.stack([cos_part, sin_part], axis=-1).reshape(wave_in.shape).astype(BF16)


def by_collectives(wide, narrow, coef, velocity, slope_y):
    gz_size, gx_size = slope_y.shape[1] * wide, slope_y.shape[2]
    kz_size, kx_size = coef.shape[1] * narrow, coef.shape[2] * wide
    values, slopes = z_tables(gz_size, kz_size)
    basis = x_table(gx_size, kx_size)
    einsum = functools.partial(jnp.einsum, preferred_element_type=F32)
    swap = functools.partial(lax.all_to_all, tiled=True)
    plane = swap(coef, "narrow", split_axis=0, concat_axis=1)
    wave_val = einsum("jn,ynk->yjk", values, plane).astype(BF16)
    wave_dz = einsum("jn,ynk->yjk", slopes, plane).astype(BF16)
    wave_val = swap(wave_val, "wide", split_axis=1, concat_axis=2)
    wave_dz = swap(wave_dz, "wide", split_axis=1, concat_axis=2)
    grid_val, grid_dx, grid_dz = (
        einsum("yjk,gk->yjg", field, basis)
        for field in (wave_val, x_slope(wave_val, gx_size), wave_dz)
    )
    total = velocity[0] * grid_dx + velocity[1] * slope_y.astype(F32) + velocity[2] * grid_dz
    half_coef = einsum("yjg,gk->yjk", (-total).astype(BF16), basis).astype(BF16)
    half_coef = swap(half_coef, "wide", split_axis=2, concat_axis=1)
    coef_z = einsum("jn,yjk->ynk", values, half_coef).astype(BF16)
    advect = swap(coef_z, "narrow", split_axis=1, concat_axis=0)
    return advect, grid_val.astype(BF16)


def solution(mesh):
    wide, narrow = mesh.shape["wide"], mesh.shape["narrow"]

    def on_device(coef, velocity, slope_y):
        whole_tiles = (
            slope_y.shape[0] == 1
            and coef.shape[1] % 16 == 0
            and coef.shape[2] == LANES
            and slope_y.shape[1] % 16 == 0
            and slope_y.shape[2] % 512 == 0
            and wide >= 4
            and wide & (wide - 1) == 0
        )
        plan = by_kernel if whole_tiles else by_collectives
        return plan(wide, narrow, coef, velocity, slope_y)

    return jax.shard_map(
        on_device,
        mesh=mesh,
        in_specs=(
            P(None, "narrow", "wide"),
            P(None, "narrow", "wide", None),
            P("narrow", "wide", None),
        ),
        out_specs=(P(None, "narrow", "wide"), P("narrow", "wide", None)),
        check_vma=False,
    )
```

```python
import functools
import math

import jax
import jax.numpy as jnp
import ml_dtypes
import numpy as np
from jax import lax
from jax.experimental import pallas as pl
from jax.experimental.pallas import tpu as pltpu
from jax.sharding import PartitionSpec as P

MESH = pl.DeviceIdType.MESH
F32 = jnp.float32
BF16 = jnp.bfloat16
LANES = 128
VMEM_BYTES = 64 * 1024 * 1024 - 256 * 1024


def x_table(gx_size, kx_size):
    points = np.arange(gx_size, dtype=np.int32)[:, None]
    column_id = np.arange(kx_size, dtype=np.int32)[None, :]
    harmonic = column_id // 2
    angles = (harmonic * points % gx_size).astype(np.float32) * np.float32(2.0 * math.pi / gx_size)
    weights = np.where(
        harmonic == 0, math.sqrt(1.0 / gx_size), math.sqrt(2.0 / gx_size)
    ).astype(np.float32)
    raw = np.where(column_id % 2 == 0, np.cos(angles), np.sin(angles))
    return (raw * weights).astype(ml_dtypes.bfloat16)


def z_tables(gz_size, kz_size):
    nodes = np.arange(gz_size, dtype=np.int32)[:, None]
    degree = np.arange(kz_size, dtype=np.int32)[None, :]
    step = np.float32(math.pi / (2.0 * gz_size))
    angles = (degree * (2 * nodes + 1) % (4 * gz_size)).astype(np.float32) * step
    polar = (2 * nodes + 1).astype(np.float32) * step
    weights = np.where(
        degree == 0, math.sqrt(1.0 / gz_size), math.sqrt(2.0 / gz_size)
    ).astype(np.float32)
    values = weights * np.cos(angles)
    slopes = weights * np.float32(2.0 / gz_size) * degree.astype(np.float32)
    slopes = slopes * np.sin(angles) / np.sin(polar)
    return values.astype(ml_dtypes.bfloat16), slopes.astype(ml_dtypes.bfloat16)


def dot(left, right):
    return jnp.dot(left, right, preferred_element_type=F32)


def flip_bits(index, mask, size):
    total, bit = 0, 1
    while bit < size:
        digit = lax.rem(lax.div(index, bit), 2)
        total = total + bit * (1 - digit if mask & bit else digit)
        bit *= 2
    return total


def kernel(
    wide, narrow, rows, gx_size,
    coef, velocity, slope_y, zt_hbm, bt_hbm, b_hbm, vt_hbm,
    advect_out, grid_out,
    zt, bt, b, vt, speed, dy,
    recv_a, send_b, recv_b, acc, adv, buoy, send_e, recv_e, send_f,
    local_sem, a_send, a_recv, b_send, b_recv, e_send, e_recv, f_send, f_recv,
):
    pairs = wide // 2
    w = lax.axis_index("wide")
    m = lax.axis_index("narrow")
    mine = lax.div(w, 2)
    beside = 2 * mine + 1 - lax.rem(w, 2)
    narrow_peers = [lax.rem(m + r, narrow) for r in range(1, narrow)]
    pair_of = [flip_bits(mine, t, pairs) for t in range(pairs)]
    far_first = list(range(pairs - 1, 0, -1))

    own = pltpu.make_async_copy(coef.at[m], recv_a.at[m], local_sem.at[0])
    own.start()
    loads = [
        pltpu.make_async_copy(src, dst, local_sem.at[1 + i])
        for i, (src, dst) in enumerate(
            [(zt_hbm, zt), (bt_hbm, bt), (velocity, speed), (slope_y, dy), (b_hbm, b), (vt_hbm, vt)]
        )
    ]
    for load in loads:
        load.start()

    barrier = pltpu.get_barrier_semaphore()
    for peer in narrow_peers:
        pl.semaphore_signal(barrier, inc=1, device_id={"narrow": peer}, device_id_type=MESH)
    for t in range(1, wide):
        pl.semaphore_signal(
            barrier, inc=1, device_id={"wide": lax.rem(w + t, wide)}, device_id_type=MESH
        )
    pl.semaphore_wait(barrier, narrow + wide - 2)

    sends = []

    def push(src, dst, send_sem, recv_sem, target):
        copy = pltpu.make_async_remote_copy(
            src_ref=src, dst_ref=dst, send_sem=send_sem, recv_sem=recv_sem,
            device_id=target, device_id_type=MESH,
        )
        copy.start()
        sends.append(copy)

    def arrived(dst, recv_sem, send_sem, target):
        pltpu.make_async_remote_copy(
            src_ref=dst, dst_ref=dst, send_sem=send_sem, recv_sem=recv_sem,
            device_id=target, device_id_type=MESH,
        ).wait_recv()

    for peer in narrow_peers:
        push(coef.at[peer], recv_a.at[m], a_send.at[peer], a_recv.at[m], {"narrow": peer})
    own.wait()
    loads[0].wait()
    for peer in narrow_peers:
        arrived(recv_a.at[peer], a_recv.at[peer], a_send.at[peer], {"narrow": peer})

    plane = recv_a[...].reshape(-1, LANES)

    def send_points(d):
        send_b[d] = dot(zt[d], plane).astype(BF16)
        push(send_b.at[d], recv_b.at[w], b_send.at[d], b_recv.at[w], {"wide": d})

    for t in far_first:
        send_points(2 * pair_of[t])
        send_points(2 * pair_of[t] + 1)
    send_points(beside)
    recv_b[w] = dot(zt[w], plane).astype(BF16)

    lane = lax.broadcasted_iota(jnp.int32, (1, LANES), 1)
    even = lax.rem(lane, 2) == 0

    def slope_of(field, first):
        harmonic = (lax.div(lane, 2) + first).astype(F32)
        rate = harmonic * (2.0 * math.pi / gx_size)
        wide_field = field.astype(F32)
        after = pltpu.roll(wide_field, LANES - 1, 1)
        before = pltpu.roll(wide_field, 1, 1)
        return jnp.where(even, rate * after, -rate * before).astype(BF16)

    def stacked(pair):
        fields = []
        for s in (0, 1):
            block = recv_b[2 * pair + s]
            val, dz = block[:rows], block[rows:]
            dx = slope_of(val, (2 * pair + s) * (LANES // 2))
            fields.append(jnp.concatenate([val, dx, dz], axis=0))
        return jnp.concatenate(fields, axis=1)

    tile = 512
    cuts = [slice(c, c + tile) for c in range(0, gx_size, tile)]
    for t in range(pairs):
        pair = pair_of[t]
        if t == 0:
            arrived(recv_b.at[beside], b_recv.at[beside], b_send.at[beside], {"wide": beside})
            loads[1].wait()
        else:
            for d in (2 * pair, 2 * pair + 1):
                arrived(recv_b.at[d], b_recv.at[d], b_send.at[d], {"wide": d})
        fields = stacked(pair)
        if t == pairs - 1:
            loads[2].wait()
            loads[3].wait()
        for cut in cuts:
            part = dot(fields, bt[pair, :, cut])
            if t > 0:
                part = part + acc[:, cut]
            if t < pairs - 1:
                acc[:, cut] = part
            else:
                buoy[0, :, cut] = part[:rows].astype(BF16)
                total = speed[0, 0, :, cut].astype(F32) * part[rows : 2 * rows]
                total = total + speed[1, 0, :, cut].astype(F32) * dy[0, :, cut].astype(F32)
                total = total + speed[2, 0, :, cut].astype(F32) * part[2 * rows :]
                adv[:, cut] = (-total).astype(BF16)
    grid_copy = pltpu.make_async_copy(buoy, grid_out, local_sem.at[7])
    grid_copy.start()

    loads[4].wait()
    for t in far_first + [0]:
        pair = pair_of[t]
        half = dot(adv[...], b[pair]).astype(BF16)
        for s in (0, 1):
            send_e[2 * pair + s] = half[:, s * LANES : (s + 1) * LANES]
        for d in (2 * pair, 2 * pair + 1) if t else (beside,):
            push(send_e.at[d], recv_e.at[w], e_send.at[d], e_recv.at[w], {"wide": d})
    recv_e[w] = send_e[w]
    loads[5].wait()
    for t in range(pairs):
        for d in (2 * pair_of[t], 2 * pair_of[t] + 1) if t else (beside,):
            arrived(recv_e.at[d], e_recv.at[d], e_send.at[d], {"wide": d})

    points = recv_e[...].reshape(-1, LANES)
    for peer in narrow_peers:
        send_f[peer] = dot(vt[peer], points).astype(BF16)
        push(send_f.at[peer], advect_out.at[m], f_send.at[peer], f_recv.at[m], {"narrow": peer})
    send_f[m] = dot(vt[m], points).astype(BF16)
    kept = pltpu.make_async_copy(send_f.at[m], advect_out.at[m], local_sem.at[8])
    kept.start()
    for peer in narrow_peers:
        arrived(advect_out.at[peer], f_recv.at[peer], f_send.at[peer], {"narrow": peer})
    kept.wait()
    grid_copy.wait()
    for copy in sends:
        copy.wait_send()


def hand_over(advect, grid, advect_out, grid_out, sem):
    copies = [
        pltpu.make_async_copy(advect, advect_out, sem.at[0]),
        pltpu.make_async_copy(grid, grid_out, sem.at[1]),
    ]
    for copy in copies:
        copy.start()
    for copy in copies:
        copy.wait()


def by_kernel(wide, narrow, coef, velocity, slope_y):
    degrees = coef.shape[1]
    rows, gx_size = slope_y.shape[1:]
    kz_size, kx_size, gz_size = degrees * narrow, LANES * wide, rows * wide
    pairs = wide // 2
    values, slopes = z_tables(gz_size, kz_size)
    basis = x_table(gx_size, kx_size)
    zt = np.concatenate(
        [values.reshape(wide, rows, kz_size), slopes.reshape(wide, rows, kz_size)], axis=1
    )
    bt = np.ascontiguousarray(basis.T).reshape(pairs, 2 * LANES, gx_size)
    b = np.ascontiguousarray(basis.reshape(gx_size, pairs, 2 * LANES).transpose(1, 0, 2))
    vt = np.ascontiguousarray(values.T).reshape(narrow, degrees, gz_size)
    hbm = pl.BlockSpec(memory_space=pltpu.HBM)
    dma = pltpu.SemaphoreType.DMA
    advect, grid = pl.pallas_call(
        functools.partial(kernel, wide, narrow, rows, gx_size),
        out_shape=(
            jax.ShapeDtypeStruct(coef.shape, BF16),
            jax.ShapeDtypeStruct(slope_y.shape, BF16),
        ),
        in_specs=[hbm] * 7,
        out_specs=(hbm, hbm),
        scratch_shapes=[
            pltpu.VMEM(zt.shape, BF16),
            pltpu.VMEM(bt.shape, BF16),
            pltpu.VMEM(b.shape, BF16),
            pltpu.VMEM(vt.shape, BF16),
            pltpu.VMEM(velocity.shape, BF16),
            pltpu.VMEM(slope_y.shape, BF16),
            pltpu.VMEM((narrow, degrees, LANES), BF16),
            pltpu.VMEM((wide, 2 * rows, LANES), BF16),
            pltpu.VMEM((wide, 2 * rows, LANES), BF16),
            pltpu.VMEM((3 * rows, gx_size), F32),
            pltpu.VMEM((rows, gx_size), BF16),
            pltpu.VMEM(slope_y.shape, BF16),
            pltpu.VMEM((wide, rows, LANES), BF16),
            pltpu.VMEM((wide, rows, LANES), BF16),
            pltpu.VMEM((narrow, degrees, LANES), BF16),
            dma((9,)),
            dma((narrow,)),
            dma((narrow,)),
            dma((wide,)),
            dma((wide,)),
            dma((wide,)),
            dma((wide,)),
            dma((narrow,)),
            dma((narrow,)),
        ],
        compiler_params=pltpu.CompilerParams(
            collective_id=0, has_side_effects=True, vmem_limit_bytes=VMEM_BYTES
        ),
    )(coef, velocity, slope_y, zt, bt, b, vt)
    return pl.pallas_call(
        hand_over,
        out_shape=(
            jax.ShapeDtypeStruct(coef.shape, BF16),
            jax.ShapeDtypeStruct(slope_y.shape, BF16),
        ),
        in_specs=[hbm] * 2,
        out_specs=(hbm, hbm),
        scratch_shapes=[dma((2,))],
        compiler_params=pltpu.CompilerParams(vmem_limit_bytes=VMEM_BYTES),
    )(advect, grid)


def x_slope(wave_in, gx_size):
    width_now = wave_in.shape[-1]
    paired = wave_in.astype(F32).reshape(wave_in.shape[:-1] + (width_now // 2, 2))
    harmonic = lax.iota(jnp.int32, width_now // 2).astype(F32)
    omega_rate = harmonic * (2.0 * math.pi / gx_size)
    cos_part = omega_rate * paired[..., 1]
    sin_part = -omega_rate * paired[..., 0]
    return jnp.stack([cos_part, sin_part], axis=-1).reshape(wave_in.shape).astype(BF16)


def by_collectives(wide, narrow, coef, velocity, slope_y):
    gz_size, gx_size = slope_y.shape[1] * wide, slope_y.shape[2]
    kz_size, kx_size = coef.shape[1] * narrow, coef.shape[2] * wide
    values, slopes = z_tables(gz_size, kz_size)
    basis = x_table(gx_size, kx_size)
    einsum = functools.partial(jnp.einsum, preferred_element_type=F32)
    swap = functools.partial(lax.all_to_all, tiled=True)
    plane = swap(coef, "narrow", split_axis=0, concat_axis=1)
    wave_val = einsum("jn,ynk->yjk", values, plane).astype(BF16)
    wave_dz = einsum("jn,ynk->yjk", slopes, plane).astype(BF16)
    wave_val = swap(wave_val, "wide", split_axis=1, concat_axis=2)
    wave_dz = swap(wave_dz, "wide", split_axis=1, concat_axis=2)
    grid_val, grid_dx, grid_dz = (
        einsum("yjk,gk->yjg", field, basis)
        for field in (wave_val, x_slope(wave_val, gx_size), wave_dz)
    )
    total = velocity[0] * grid_dx + velocity[1] * slope_y.astype(F32) + velocity[2] * grid_dz
    half_coef = einsum("yjg,gk->yjk", (-total).astype(BF16), basis).astype(BF16)
    half_coef = swap(half_coef, "wide", split_axis=2, concat_axis=1)
    coef_z = einsum("jn,yjk->ynk", values, half_coef).astype(BF16)
    advect = swap(coef_z, "narrow", split_axis=1, concat_axis=0)
    return advect, grid_val.astype(BF16)


def solution(mesh):
    wide, narrow = mesh.shape["wide"], mesh.shape["narrow"]

    def on_device(coef, velocity, slope_y):
        whole_tiles = (
            slope_y.shape[0] == 1
            and coef.shape[1] % 16 == 0
            and coef.shape[2] == LANES
            and slope_y.shape[1] % 16 == 0
            and slope_y.shape[2] % 512 == 0
            and wide >= 4
            and wide & (wide - 1) == 0
        )
        plan = by_kernel if whole_tiles else by_collectives
        return plan(wide, narrow, coef, velocity, slope_y)

    return jax.shard_map(
        on_device,
        mesh=mesh,
        in_specs=(
            P(None, "narrow", "wide"),
            P(None, "narrow", "wide", None),
            P("narrow", "wide", None),
        ),
        out_specs=(P(None, "narrow", "wide"), P("narrow", "wide", None)),
        check_vma=False,
    )
```

```python
import functools
import math

import jax
import jax.numpy as jnp
import ml_dtypes
import numpy as np
from jax import lax
from jax.experimental import pallas as pl
from jax.experimental.pallas import tpu as pltpu
from jax.sharding import PartitionSpec as P

MESH = pl.DeviceIdType.MESH
F32 = jnp.float32
BF16 = jnp.bfloat16
LANES = 128
VMEM_BYTES = 64 * 1024 * 1024 - 256 * 1024


def x_table(gx_size, kx_size):
    points = np.arange(gx_size, dtype=np.int32)[:, None]
    column_id = np.arange(kx_size, dtype=np.int32)[None, :]
    harmonic = column_id // 2
    angles = (harmonic * points % gx_size).astype(np.float32) * np.float32(2.0 * math.pi / gx_size)
    weights = np.where(
        harmonic == 0, math.sqrt(1.0 / gx_size), math.sqrt(2.0 / gx_size)
    ).astype(np.float32)
    raw = np.where(column_id % 2 == 0, np.cos(angles), np.sin(angles))
    return (raw * weights).astype(ml_dtypes.bfloat16)


def z_tables(gz_size, kz_size):
    nodes = np.arange(gz_size, dtype=np.int32)[:, None]
    degree = np.arange(kz_size, dtype=np.int32)[None, :]
    step = np.float32(math.pi / (2.0 * gz_size))
    angles = (degree * (2 * nodes + 1) % (4 * gz_size)).astype(np.float32) * step
    polar = (2 * nodes + 1).astype(np.float32) * step
    weights = np.where(
        degree == 0, math.sqrt(1.0 / gz_size), math.sqrt(2.0 / gz_size)
    ).astype(np.float32)
    values = weights * np.cos(angles)
    slopes = weights * np.float32(2.0 / gz_size) * degree.astype(np.float32)
    slopes = slopes * np.sin(angles) / np.sin(polar)
    return values.astype(ml_dtypes.bfloat16), slopes.astype(ml_dtypes.bfloat16)


def dot(left, right):
    return jnp.dot(left, right, preferred_element_type=F32)


def dot_last(left, right):
    return lax.dot_general(left, right, (((1,), (1,)), ((), ())), preferred_element_type=F32)


def flip_bits(index, mask, size):
    total, bit = 0, 1
    while bit < size:
        digit = lax.rem(lax.div(index, bit), 2)
        total = total + bit * (1 - digit if mask & bit else digit)
        bit *= 2
    return total


def kernel(
    wide, narrow, rows, gx_size,
    coef, velocity, slope_y, zt_hbm, bt_hbm, vt_hbm,
    advect_out, grid_out,
    zt, bt, vt, speed, dy,
    recv_a, send_b, recv_b, acc, adv, buoy, send_e, recv_e, send_f,
    local_sem, a_send, a_recv, b_send, b_recv, e_send, e_recv, f_send, f_recv,
):
    pairs = wide // 2
    w = lax.axis_index("wide")
    m = lax.axis_index("narrow")
    mine = lax.div(w, 2)
    beside = 2 * mine + 1 - lax.rem(w, 2)
    narrow_peers = [lax.rem(m + r, narrow) for r in range(1, narrow)]
    pair_of = [flip_bits(mine, t, pairs) for t in range(pairs)]
    far_first = list(range(pairs - 1, 0, -1))

    own = pltpu.make_async_copy(coef.at[m], recv_a.at[m], local_sem.at[0])
    own.start()
    loads = [
        pltpu.make_async_copy(src, dst, local_sem.at[1 + i])
        for i, (src, dst) in enumerate(
            [(zt_hbm, zt), (bt_hbm, bt), (velocity, speed), (slope_y, dy), (vt_hbm, vt)]
        )
    ]
    for load in loads[:2]:
        load.start()

    barrier = pltpu.get_barrier_semaphore()
    for peer in narrow_peers:
        pl.semaphore_signal(barrier, inc=1, device_id={"narrow": peer}, device_id_type=MESH)
    for t in range(1, wide):
        pl.semaphore_signal(
            barrier, inc=1, device_id={"wide": lax.rem(w + t, wide)}, device_id_type=MESH
        )
    pl.semaphore_wait(barrier, narrow + wide - 2)

    sends = []

    def push(src, dst, send_sem, recv_sem, target):
        copy = pltpu.make_async_remote_copy(
            src_ref=src, dst_ref=dst, send_sem=send_sem, recv_sem=recv_sem,
            device_id=target, device_id_type=MESH,
        )
        copy.start()
        sends.append(copy)

    def arrived(dst, recv_sem, send_sem, target):
        pltpu.make_async_remote_copy(
            src_ref=dst, dst_ref=dst, send_sem=send_sem, recv_sem=recv_sem,
            device_id=target, device_id_type=MESH,
        ).wait_recv()

    for peer in narrow_peers:
        push(coef.at[peer], recv_a.at[m], a_send.at[peer], a_recv.at[m], {"narrow": peer})
    own.wait()
    loads[0].wait()
    for peer in narrow_peers:
        arrived(recv_a.at[peer], a_recv.at[peer], a_send.at[peer], {"narrow": peer})

    plane = recv_a[...].reshape(-1, LANES)

    def send_points(d):
        send_b[d] = dot(zt[d], plane).astype(BF16)
        push(send_b.at[d], recv_b.at[w], b_send.at[d], b_recv.at[w], {"wide": d})

    for t in far_first:
        send_points(2 * pair_of[t])
        send_points(2 * pair_of[t] + 1)
    send_points(beside)
    for load in loads[2:]:
        load.start()
    recv_b[w] = dot(zt[w], plane).astype(BF16)

    lane = lax.broadcasted_iota(jnp.int32, (1, LANES), 1)
    even = lax.rem(lane, 2) == 0

    def slope_of(field, first):
        harmonic = (lax.div(lane, 2) + first).astype(F32)
        rate = harmonic * (2.0 * math.pi / gx_size)
        wide_field = field.astype(F32)
        after = pltpu.roll(wide_field, LANES - 1, 1)
        before = pltpu.roll(wide_field, 1, 1)
        return jnp.where(even, rate * after, -rate * before).astype(BF16)

    def stacked(pair):
        fields = []
        for s in (0, 1):
            block = recv_b[2 * pair + s]
            val, dz = block[:rows], block[rows:]
            dx = slope_of(val, (2 * pair + s) * (LANES // 2))
            fields.append(jnp.concatenate([val, dx, dz], axis=0))
        return jnp.concatenate(fields, axis=1)

    tile = 512
    cuts = [slice(c, c + tile) for c in range(0, gx_size, tile)]
    for t in range(pairs):
        pair = pair_of[t]
        if t == 0:
            arrived(recv_b.at[beside], b_recv.at[beside], b_send.at[beside], {"wide": beside})
            loads[1].wait()
        else:
            for d in (2 * pair, 2 * pair + 1):
                arrived(recv_b.at[d], b_recv.at[d], b_send.at[d], {"wide": d})
        fields = stacked(pair)
        if t == pairs - 1:
            loads[2].wait()
            loads[3].wait()
        for cut in cuts:
            part = dot(fields, bt[pair, :, cut])
            if t > 0:
                part = part + acc[:, cut]
            if t < pairs - 1:
                acc[:, cut] = part
            else:
                buoy[0, :, cut] = part[:rows].astype(BF16)
                total = speed[0, 0, :, cut].astype(F32) * part[rows : 2 * rows]
                total = total + speed[1, 0, :, cut].astype(F32) * dy[0, :, cut].astype(F32)
                total = total + speed[2, 0, :, cut].astype(F32) * part[2 * rows :]
                adv[:, cut] = (-total).astype(BF16)
    grid_copy = pltpu.make_async_copy(buoy, grid_out, local_sem.at[6])
    grid_copy.start()

    for t in far_first + [0]:
        pair = pair_of[t]
        half = dot_last(adv[...], bt[pair]).astype(BF16)
        for s in (0, 1):
            send_e[2 * pair + s] = half[:, s * LANES : (s + 1) * LANES]
        for d in (2 * pair, 2 * pair + 1) if t else (beside,):
            push(send_e.at[d], recv_e.at[w], e_send.at[d], e_recv.at[w], {"wide": d})
    recv_e[w] = send_e[w]
    loads[4].wait()
    for t in range(pairs):
        for d in (2 * pair_of[t], 2 * pair_of[t] + 1) if t else (beside,):
            arrived(recv_e.at[d], e_recv.at[d], e_send.at[d], {"wide": d})

    points = recv_e[...].reshape(-1, LANES)
    for peer in narrow_peers:
        send_f[peer] = dot(vt[peer], points).astype(BF16)
        push(send_f.at[peer], advect_out.at[m], f_send.at[peer], f_recv.at[m], {"narrow": peer})
    send_f[m] = dot(vt[m], points).astype(BF16)
    kept = pltpu.make_async_copy(send_f.at[m], advect_out.at[m], local_sem.at[7])
    kept.start()
    for peer in narrow_peers:
        arrived(advect_out.at[peer], f_recv.at[peer], f_send.at[peer], {"narrow": peer})
    kept.wait()
    grid_copy.wait()
    for copy in sends:
        copy.wait_send()


def hand_over(advect, grid, advect_out, grid_out, advect_held, grid_held, sem):
    routes = [(advect, advect_held, advect_out), (grid, grid_held, grid_out)]
    fetches = [
        pltpu.make_async_copy(src, held, sem.at[i]) for i, (src, held, _) in enumerate(routes)
    ]
    stores = [
        pltpu.make_async_copy(held, dst, sem.at[2 + i]) for i, (_, held, dst) in enumerate(routes)
    ]
    for fetch in fetches:
        fetch.start()
    for fetch, store in zip(fetches, stores):
        fetch.wait()
        store.start()
    for store in stores:
        store.wait()


def by_kernel(wide, narrow, coef, velocity, slope_y):
    degrees = coef.shape[1]
    rows, gx_size = slope_y.shape[1:]
    kz_size, kx_size, gz_size = degrees * narrow, LANES * wide, rows * wide
    pairs = wide // 2
    values, slopes = z_tables(gz_size, kz_size)
    basis = x_table(gx_size, kx_size)
    zt = np.concatenate(
        [values.reshape(wide, rows, kz_size), slopes.reshape(wide, rows, kz_size)], axis=1
    )
    bt = np.ascontiguousarray(basis.T).reshape(pairs, 2 * LANES, gx_size)
    vt = np.ascontiguousarray(values.T).reshape(narrow, degrees, gz_size)
    hbm = pl.BlockSpec(memory_space=pltpu.HBM)
    dma = pltpu.SemaphoreType.DMA
    advect, grid = pl.pallas_call(
        functools.partial(kernel, wide, narrow, rows, gx_size),
        out_shape=(
            jax.ShapeDtypeStruct(coef.shape, BF16),
            jax.ShapeDtypeStruct(slope_y.shape, BF16),
        ),
        in_specs=[hbm] * 6,
        out_specs=(hbm, hbm),
        scratch_shapes=[
            pltpu.VMEM(zt.shape, BF16),
            pltpu.VMEM(bt.shape, BF16),
            pltpu.VMEM(vt.shape, BF16),
            pltpu.VMEM(velocity.shape, BF16),
            pltpu.VMEM(slope_y.shape, BF16),
            pltpu.VMEM((narrow, degrees, LANES), BF16),
            pltpu.VMEM((wide, 2 * rows, LANES), BF16),
            pltpu.VMEM((wide, 2 * rows, LANES), BF16),
            pltpu.VMEM((3 * rows, gx_size), F32),
            pltpu.VMEM((rows, gx_size), BF16),
            pltpu.VMEM(slope_y.shape, BF16),
            pltpu.VMEM((wide, rows, LANES), BF16),
            pltpu.VMEM((wide, rows, LANES), BF16),
            pltpu.VMEM((narrow, degrees, LANES), BF16),
            dma((8,)),
            dma((narrow,)),
            dma((narrow,)),
            dma((wide,)),
            dma((wide,)),
            dma((wide,)),
            dma((wide,)),
            dma((narrow,)),
            dma((narrow,)),
        ],
        compiler_params=pltpu.CompilerParams(
            collective_id=0, has_side_effects=True, vmem_limit_bytes=VMEM_BYTES
        ),
    )(coef, velocity, slope_y, zt, bt, vt)
    return pl.pallas_call(
        hand_over,
        out_shape=(
            jax.ShapeDtypeStruct(coef.shape, BF16),
            jax.ShapeDtypeStruct(slope_y.shape, BF16),
        ),
        in_specs=[hbm] * 2,
        out_specs=(hbm, hbm),
        scratch_shapes=[
            pltpu.VMEM(coef.shape, BF16),
            pltpu.VMEM(slope_y.shape, BF16),
            dma((4,)),
        ],
        compiler_params=pltpu.CompilerParams(vmem_limit_bytes=VMEM_BYTES),
    )(advect, grid)


def x_slope(wave_in, gx_size):
    width_now = wave_in.shape[-1]
    paired = wave_in.astype(F32).reshape(wave_in.shape[:-1] + (width_now // 2, 2))
    harmonic = lax.iota(jnp.int32, width_now // 2).astype(F32)
    omega_rate = harmonic * (2.0 * math.pi / gx_size)
    cos_part = omega_rate * paired[..., 1]
    sin_part = -omega_rate * paired[..., 0]
    return jnp.stack([cos_part, sin_part], axis=-1).reshape(wave_in.shape).astype(BF16)


def by_collectives(wide, narrow, coef, velocity, slope_y):
    gz_size, gx_size = slope_y.shape[1] * wide, slope_y.shape[2]
    kz_size, kx_size = coef.shape[1] * narrow, coef.shape[2] * wide
    values, slopes = z_tables(gz_size, kz_size)
    basis = x_table(gx_size, kx_size)
    einsum = functools.partial(jnp.einsum, preferred_element_type=F32)
    swap = functools.partial(lax.all_to_all, tiled=True)
    plane = swap(coef, "narrow", split_axis=0, concat_axis=1)
    wave_val = einsum("jn,ynk->yjk", values, plane).astype(BF16)
    wave_dz = einsum("jn,ynk->yjk", slopes, plane).astype(BF16)
    wave_val = swap(wave_val, "wide", split_axis=1, concat_axis=2)
    wave_dz = swap(wave_dz, "wide", split_axis=1, concat_axis=2)
    grid_val, grid_dx, grid_dz = (
        einsum("yjk,gk->yjg", field, basis)
        for field in (wave_val, x_slope(wave_val, gx_size), wave_dz)
    )
    total = velocity[0] * grid_dx + velocity[1] * slope_y.astype(F32) + velocity[2] * grid_dz
    half_coef = einsum("yjg,gk->yjk", (-total).astype(BF16), basis).astype(BF16)
    half_coef = swap(half_coef, "wide", split_axis=2, concat_axis=1)
    coef_z = einsum("jn,yjk->ynk", values, half_coef).astype(BF16)
    advect = swap(coef_z, "narrow", split_axis=1, concat_axis=0)
    return advect, grid_val.astype(BF16)


def solution(mesh):
    wide, narrow = mesh.shape["wide"], mesh.shape["narrow"]

    def on_device(coef, velocity, slope_y):
        whole_tiles = (
            slope_y.shape[0] == 1
            and coef.shape[1] % 16 == 0
            and coef.shape[2] == LANES
            and slope_y.shape[1] % 16 == 0
            and slope_y.shape[2] % 512 == 0
            and wide >= 4
            and wide & (wide - 1) == 0
        )
        plan = by_kernel if whole_tiles else by_collectives
        return plan(wide, narrow, coef, velocity, slope_y)

    return jax.shard_map(
        on_device,
        mesh=mesh,
        in_specs=(
            P(None, "narrow", "wide"),
            P(None, "narrow", "wide", None),
            P("narrow", "wide", None),
        ),
        out_specs=(P(None, "narrow", "wide"), P("narrow", "wide", None)),
        check_vma=False,
    )
```

```python
import functools
import math

import jax
import jax.numpy as jnp
import ml_dtypes
import numpy as np
from jax import lax
from jax.experimental import pallas as pl
from jax.experimental.pallas import tpu as pltpu
from jax.sharding import PartitionSpec as P

MESH = pl.DeviceIdType.MESH
F32 = jnp.float32
BF16 = jnp.bfloat16
LANES = 128
VMEM_BYTES = 64 * 1024 * 1024 - 256 * 1024


def x_table(gx_size, kx_size):
    points = np.arange(gx_size, dtype=np.int32)[:, None]
    column_id = np.arange(kx_size, dtype=np.int32)[None, :]
    harmonic = column_id // 2
    angles = (harmonic * points % gx_size).astype(np.float32) * np.float32(2.0 * math.pi / gx_size)
    weights = np.where(
        harmonic == 0, math.sqrt(1.0 / gx_size), math.sqrt(2.0 / gx_size)
    ).astype(np.float32)
    raw = np.where(column_id % 2 == 0, np.cos(angles), np.sin(angles))
    return (raw * weights).astype(ml_dtypes.bfloat16)


def z_tables(gz_size, kz_size):
    nodes = np.arange(gz_size, dtype=np.int32)[:, None]
    degree = np.arange(kz_size, dtype=np.int32)[None, :]
    step = np.float32(math.pi / (2.0 * gz_size))
    angles = (degree * (2 * nodes + 1) % (4 * gz_size)).astype(np.float32) * step
    polar = (2 * nodes + 1).astype(np.float32) * step
    weights = np.where(
        degree == 0, math.sqrt(1.0 / gz_size), math.sqrt(2.0 / gz_size)
    ).astype(np.float32)
    values = weights * np.cos(angles)
    slopes = weights * np.float32(2.0 / gz_size) * degree.astype(np.float32)
    slopes = slopes * np.sin(angles) / np.sin(polar)
    return values.astype(ml_dtypes.bfloat16), slopes.astype(ml_dtypes.bfloat16)


def dot(left, right):
    return jnp.dot(left, right, preferred_element_type=F32)


def dot_last(left, right):
    return lax.dot_general(left, right, (((1,), (1,)), ((), ())), preferred_element_type=F32)


def flip_bits(index, mask, size):
    total, bit = 0, 1
    while bit < size:
        digit = lax.rem(lax.div(index, bit), 2)
        total = total + bit * (1 - digit if mask & bit else digit)
        bit *= 2
    return total


def kernel(
    wide, narrow, groups, gx_size,
    coef, velocity, slope_y, zt_hbm, bt_hbm, vt_hbm,
    advect_out, grid_out,
    zt, bt, vt, speed, dy,
    recv_a, send_b, recv_b, acc, adv, buoy, send_e, recv_e, send_f,
    local_sem, a_send, a_recv, b_send, b_recv, e_send, e_recv, f_send, f_recv,
):
    pairs = wide // 2
    w = lax.axis_index("wide")
    m = lax.axis_index("narrow")
    mine = lax.div(w, 2)
    beside = 2 * mine + 1 - lax.rem(w, 2)
    narrow_peers = [lax.rem(m + r, narrow) for r in range(1, narrow)]
    pair_of = [flip_bits(mine, t, pairs) for t in range(pairs)]
    far_first = list(range(pairs - 1, 0, -1))

    def others(t):
        return (2 * pair_of[t], 2 * pair_of[t] + 1) if t else (beside,)

    own = pltpu.make_async_copy(coef.at[m], recv_a.at[m], local_sem.at[0])
    own.start()
    loads = [
        pltpu.make_async_copy(src, dst, local_sem.at[1 + i])
        for i, (src, dst) in enumerate(
            [(zt_hbm, zt), (bt_hbm, bt), (velocity, speed), (slope_y, dy), (vt_hbm, vt)]
        )
    ]
    for load in loads[:2]:
        load.start()

    barrier = pltpu.get_barrier_semaphore()
    for peer in narrow_peers:
        pl.semaphore_signal(barrier, inc=1, device_id={"narrow": peer}, device_id_type=MESH)
    for t in range(1, wide):
        pl.semaphore_signal(
            barrier, inc=1, device_id={"wide": lax.rem(w + t, wide)}, device_id_type=MESH
        )
    pl.semaphore_wait(barrier, narrow + wide - 2)

    sends = []

    def push(src, dst, send_sem, recv_sem, target):
        copy = pltpu.make_async_remote_copy(
            src_ref=src, dst_ref=dst, send_sem=send_sem, recv_sem=recv_sem,
            device_id=target, device_id_type=MESH,
        )
        copy.start()
        sends.append(copy)

    def arrived(dst, recv_sem, send_sem, target):
        pltpu.make_async_remote_copy(
            src_ref=dst, dst_ref=dst, send_sem=send_sem, recv_sem=recv_sem,
            device_id=target, device_id_type=MESH,
        ).wait_recv()

    for peer in narrow_peers:
        push(coef.at[peer], recv_a.at[m], a_send.at[peer], a_recv.at[m], {"narrow": peer})
    own.wait()
    loads[0].wait()
    for peer in narrow_peers:
        arrived(recv_a.at[peer], a_recv.at[peer], a_send.at[peer], {"narrow": peer})

    plane = recv_a[...].reshape(-1, LANES)

    def of_group(g):
        return pl.ds(2 * groups[g][0], 2 * groups[g][1])

    def points_at(d, g):
        return dot(zt[d, of_group(g)], plane).astype(BF16)

    for g in range(len(groups)):
        for t in far_first + [0]:
            for d in others(t):
                send_b[d, of_group(g)] = points_at(d, g)
                push(
                    send_b.at[d, of_group(g)], recv_b.at[w, of_group(g)],
                    b_send.at[g, d], b_recv.at[g, w], {"wide": d},
                )
        recv_b[w, of_group(g)] = points_at(w, g)
    for load in loads[2:]:
        load.start()

    lane = lax.broadcasted_iota(jnp.int32, (1, LANES), 1)
    even = lax.rem(lane, 2) == 0

    def slope_of(field, first):
        harmonic = (lax.div(lane, 2) + first).astype(F32)
        rate = harmonic * (2.0 * math.pi / gx_size)
        wide_field = field.astype(F32)
        after = pltpu.roll(wide_field, LANES - 1, 1)
        before = pltpu.roll(wide_field, 1, 1)
        return jnp.where(even, rate * after, -rate * before).astype(BF16)

    def stacked(pair, g):
        count = groups[g][1]
        fields = []
        for s in (0, 1):
            block = recv_b[2 * pair + s, of_group(g)]
            val, dz = block[:count], block[count:]
            dx = slope_of(val, (2 * pair + s) * (LANES // 2))
            fields.append(jnp.concatenate([val, dx, dz], axis=0))
        return jnp.concatenate(fields, axis=1)

    tile = 512
    cuts = [slice(c, c + tile) for c in range(0, gx_size, tile)]
    for g, (first, count) in enumerate(groups):
        rows = slice(first, first + count)
        for t in range(pairs):
            pair = pair_of[t]
            for d in others(t):
                arrived(
                    recv_b.at[d, of_group(g)], b_recv.at[g, d], b_send.at[g, d], {"wide": d}
                )
            fields = stacked(pair, g)
            if g == 0 and t == 0:
                loads[1].wait()
            if g == 0 and t == pairs - 1:
                loads[2].wait()
                loads[3].wait()
            for cut in cuts:
                part = dot(fields, bt[pair, :, cut])
                if t > 0:
                    part = part + acc[: 3 * count, cut]
                if t < pairs - 1:
                    acc[: 3 * count, cut] = part
                else:
                    buoy[0, rows, cut] = part[:count].astype(BF16)
                    total = speed[0, 0, rows, cut].astype(F32) * part[count : 2 * count]
                    total = total + speed[1, 0, rows, cut].astype(F32) * dy[0, rows, cut].astype(F32)
                    total = total + speed[2, 0, rows, cut].astype(F32) * part[2 * count :]
                    adv[rows, cut] = (-total).astype(BF16)

        for t in far_first + [0]:
            pair = pair_of[t]
            half = dot_last(adv[rows], bt[pair]).astype(BF16)
            for s in (0, 1):
                send_e[2 * pair + s, rows] = half[:, s * LANES : (s + 1) * LANES]
            for d in others(t):
                push(
                    send_e.at[d, pl.ds(first, count)], recv_e.at[w, pl.ds(first, count)],
                    e_send.at[g, d], e_recv.at[g, w], {"wide": d},
                )
    grid_copy = pltpu.make_async_copy(buoy, grid_out, local_sem.at[6])
    grid_copy.start()
    recv_e[w] = send_e[w]
    loads[4].wait()
    for g, (first, count) in enumerate(groups):
        for t in range(pairs):
            for d in others(t):
                arrived(
                    recv_e.at[d, pl.ds(first, count)], e_recv.at[g, d], e_send.at[g, d],
                    {"wide": d},
                )

    points = recv_e[...].reshape(-1, LANES)
    for peer in narrow_peers:
        send_f[peer] = dot(vt[peer], points).astype(BF16)
        push(send_f.at[peer], advect_out.at[m], f_send.at[peer], f_recv.at[m], {"narrow": peer})
    send_f[m] = dot(vt[m], points).astype(BF16)
    kept = pltpu.make_async_copy(send_f.at[m], advect_out.at[m], local_sem.at[7])
    kept.start()
    for peer in narrow_peers:
        arrived(advect_out.at[peer], f_recv.at[peer], f_send.at[peer], {"narrow": peer})
    kept.wait()
    grid_copy.wait()
    for copy in sends:
        copy.wait_send()


def hand_over(advect, grid, advect_out, grid_out, advect_held, grid_held, sem):
    routes = [(advect, advect_held, advect_out), (grid, grid_held, grid_out)]
    fetches = [
        pltpu.make_async_copy(src, held, sem.at[i]) for i, (src, held, _) in enumerate(routes)
    ]
    stores = [
        pltpu.make_async_copy(held, dst, sem.at[2 + i]) for i, (_, held, dst) in enumerate(routes)
    ]
    for fetch in fetches:
        fetch.start()
    for fetch, store in zip(fetches, stores):
        fetch.wait()
        store.start()
    for store in stores:
        store.wait()


def by_kernel(wide, narrow, coef, velocity, slope_y):
    degrees = coef.shape[1]
    rows, gx_size = slope_y.shape[1:]
    kz_size, kx_size, gz_size = degrees * narrow, LANES * wide, rows * wide
    pairs = wide // 2
    values, slopes = z_tables(gz_size, kz_size)
    basis = x_table(gx_size, kx_size)
    early = max(16, rows * 2 // 3 // 16 * 16)
    groups = [(0, early), (early, rows - early)] if early < rows else [(0, rows)]
    values_at = values.reshape(wide, rows, kz_size)
    slopes_at = slopes.reshape(wide, rows, kz_size)
    zt = np.concatenate(
        [
            table[:, first : first + count]
            for first, count in groups
            for table in (values_at, slopes_at)
        ],
        axis=1,
    )
    bt = np.ascontiguousarray(basis.T).reshape(pairs, 2 * LANES, gx_size)
    vt = np.ascontiguousarray(values.T).reshape(narrow, degrees, gz_size)
    hbm = pl.BlockSpec(memory_space=pltpu.HBM)
    dma = pltpu.SemaphoreType.DMA
    advect, grid = pl.pallas_call(
        functools.partial(kernel, wide, narrow, groups, gx_size),
        out_shape=(
            jax.ShapeDtypeStruct(coef.shape, BF16),
            jax.ShapeDtypeStruct(slope_y.shape, BF16),
        ),
        in_specs=[hbm] * 6,
        out_specs=(hbm, hbm),
        scratch_shapes=[
            pltpu.VMEM(zt.shape, BF16),
            pltpu.VMEM(bt.shape, BF16),
            pltpu.VMEM(vt.shape, BF16),
            pltpu.VMEM(velocity.shape, BF16),
            pltpu.VMEM(slope_y.shape, BF16),
            pltpu.VMEM((narrow, degrees, LANES), BF16),
            pltpu.VMEM((wide, 2 * rows, LANES), BF16),
            pltpu.VMEM((wide, 2 * rows, LANES), BF16),
            pltpu.VMEM((3 * groups[0][1], gx_size), F32),
            pltpu.VMEM((rows, gx_size), BF16),
            pltpu.VMEM(slope_y.shape, BF16),
            pltpu.VMEM((wide, rows, LANES), BF16),
            pltpu.VMEM((wide, rows, LANES), BF16),
            pltpu.VMEM((narrow, degrees, LANES), BF16),
            dma((8,)),
            dma((narrow,)),
            dma((narrow,)),
            dma((len(groups), wide)),
            dma((len(groups), wide)),
            dma((len(groups), wide)),
            dma((len(groups), wide)),
            dma((narrow,)),
            dma((narrow,)),
        ],
        compiler_params=pltpu.CompilerParams(
            collective_id=0, has_side_effects=True, vmem_limit_bytes=VMEM_BYTES
        ),
    )(coef, velocity, slope_y, zt, bt, vt)
    return pl.pallas_call(
        hand_over,
        out_shape=(
            jax.ShapeDtypeStruct(coef.shape, BF16),
            jax.ShapeDtypeStruct(slope_y.shape, BF16),
        ),
        in_specs=[hbm] * 2,
        out_specs=(hbm, hbm),
        scratch_shapes=[
            pltpu.VMEM(coef.shape, BF16),
            pltpu.VMEM(slope_y.shape, BF16),
            dma((4,)),
        ],
        compiler_params=pltpu.CompilerParams(vmem_limit_bytes=VMEM_BYTES),
    )(advect, grid)


def x_slope(wave_in, gx_size):
    width_now = wave_in.shape[-1]
    paired = wave_in.astype(F32).reshape(wave_in.shape[:-1] + (width_now // 2, 2))
    harmonic = lax.iota(jnp.int32, width_now // 2).astype(F32)
    omega_rate = harmonic * (2.0 * math.pi / gx_size)
    cos_part = omega_rate * paired[..., 1]
    sin_part = -omega_rate * paired[..., 0]
    return jnp.stack([cos_part, sin_part], axis=-1).reshape(wave_in.shape).astype(BF16)


def by_collectives(wide, narrow, coef, velocity, slope_y):
    gz_size, gx_size = slope_y.shape[1] * wide, slope_y.shape[2]
    kz_size, kx_size = coef.shape[1] * narrow, coef.shape[2] * wide
    values, slopes = z_tables(gz_size, kz_size)
    basis = x_table(gx_size, kx_size)
    einsum = functools.partial(jnp.einsum, preferred_element_type=F32)
    swap = functools.partial(lax.all_to_all, tiled=True)
    plane = swap(coef, "narrow", split_axis=0, concat_axis=1)
    wave_val = einsum("jn,ynk->yjk", values, plane).astype(BF16)
    wave_dz = einsum("jn,ynk->yjk", slopes, plane).astype(BF16)
    wave_val = swap(wave_val, "wide", split_axis=1, concat_axis=2)
    wave_dz = swap(wave_dz, "wide", split_axis=1, concat_axis=2)
    grid_val, grid_dx, grid_dz = (
        einsum("yjk,gk->yjg", field, basis)
        for field in (wave_val, x_slope(wave_val, gx_size), wave_dz)
    )
    total = velocity[0] * grid_dx + velocity[1] * slope_y.astype(F32) + velocity[2] * grid_dz
    half_coef = einsum("yjg,gk->yjk", (-total).astype(BF16), basis).astype(BF16)
    half_coef = swap(half_coef, "wide", split_axis=2, concat_axis=1)
    coef_z = einsum("jn,yjk->ynk", values, half_coef).astype(BF16)
    advect = swap(coef_z, "narrow", split_axis=1, concat_axis=0)
    return advect, grid_val.astype(BF16)


def solution(mesh):
    wide, narrow = mesh.shape["wide"], mesh.shape["narrow"]

    def on_device(coef, velocity, slope_y):
        whole_tiles = (
            slope_y.shape[0] == 1
            and coef.shape[1] % 16 == 0
            and coef.shape[2] == LANES
            and slope_y.shape[1] % 16 == 0
            and slope_y.shape[2] % 512 == 0
            and wide >= 4
            and wide & (wide - 1) == 0
        )
        plan = by_kernel if whole_tiles else by_collectives
        return plan(wide, narrow, coef, velocity, slope_y)

    return jax.shard_map(
        on_device,
        mesh=mesh,
        in_specs=(
            P(None, "narrow", "wide"),
            P(None, "narrow", "wide", None),
            P("narrow", "wide", None),
        ),
        out_specs=(P(None, "narrow", "wide"), P("narrow", "wide", None)),
        check_vma=False,
    )
```

```python
import functools
import math

import jax
import jax.numpy as jnp
import ml_dtypes
import numpy as np
from jax import lax
from jax.experimental import pallas as pl
from jax.experimental.pallas import tpu as pltpu
from jax.sharding import PartitionSpec as P

MESH = pl.DeviceIdType.MESH
F32 = jnp.float32
BF16 = jnp.bfloat16
LANES = 128
VMEM_BYTES = 64 * 1024 * 1024 - 256 * 1024


def x_table(gx_size, kx_size):
    points = np.arange(gx_size, dtype=np.int32)[:, None]
    column_id = np.arange(kx_size, dtype=np.int32)[None, :]
    harmonic = column_id // 2
    angles = (harmonic * points % gx_size).astype(np.float32) * np.float32(2.0 * math.pi / gx_size)
    weights = np.where(
        harmonic == 0, math.sqrt(1.0 / gx_size), math.sqrt(2.0 / gx_size)
    ).astype(np.float32)
    raw = np.where(column_id % 2 == 0, np.cos(angles), np.sin(angles))
    return (raw * weights).astype(ml_dtypes.bfloat16)


def z_tables(gz_size, kz_size):
    nodes = np.arange(gz_size, dtype=np.int32)[:, None]
    degree = np.arange(kz_size, dtype=np.int32)[None, :]
    step = np.float32(math.pi / (2.0 * gz_size))
    angles = (degree * (2 * nodes + 1) % (4 * gz_size)).astype(np.float32) * step
    polar = (2 * nodes + 1).astype(np.float32) * step
    weights = np.where(
        degree == 0, math.sqrt(1.0 / gz_size), math.sqrt(2.0 / gz_size)
    ).astype(np.float32)
    values = weights * np.cos(angles)
    slopes = weights * np.float32(2.0 / gz_size) * degree.astype(np.float32)
    slopes = slopes * np.sin(angles) / np.sin(polar)
    return values.astype(ml_dtypes.bfloat16), slopes.astype(ml_dtypes.bfloat16)


def dot(left, right):
    return jnp.dot(left, right, preferred_element_type=F32)


def dot_last(left, right):
    return lax.dot_general(left, right, (((1,), (1,)), ((), ())), preferred_element_type=F32)


def flip_bits(index, mask, size):
    total, bit = 0, 1
    while bit < size:
        digit = lax.rem(lax.div(index, bit), 2)
        total = total + bit * (1 - digit if mask & bit else digit)
        bit *= 2
    return total


def kernel(
    wide, narrow, rows, gx_size,
    coef, velocity, slope_y, order, order_back, zt_hbm, bt_hbm, vt_hbm,
    advect_out, grid_out,
    zt, bt, vt, speed, dy,
    recv_a, send_b, recv_b, acc, adv, buoy, send_e, recv_e, points, send_f,
    local_sem, a_send, a_recv, b_send, b_recv, e_send, e_recv, f_send, f_recv,
):
    pairs = wide // 2
    w = lax.axis_index("wide")
    m = lax.axis_index("narrow")
    mine = lax.div(w, 2)
    beside = 2 * mine + 1 - lax.rem(w, 2)
    narrow_peers = [lax.rem(m + r, narrow) for r in range(1, narrow)]
    pair_of = [flip_bits(mine, t, pairs) for t in range(pairs)]
    far_first = list(range(pairs - 1, 0, -1))

    own = pltpu.make_async_copy(coef.at[m], recv_a.at[m], local_sem.at[0])
    own.start()
    loads = [
        pltpu.make_async_copy(src, dst, local_sem.at[1 + i])
        for i, (src, dst) in enumerate(
            [(zt_hbm, zt), (bt_hbm, bt), (velocity, speed), (slope_y, dy), (vt_hbm, vt)]
        )
    ]
    for load in loads[:2]:
        load.start()

    barrier = pltpu.get_barrier_semaphore()
    for peer in narrow_peers:
        pl.semaphore_signal(barrier, inc=1, device_id={"narrow": peer}, device_id_type=MESH)
    for t in range(1, wide):
        pl.semaphore_signal(
            barrier, inc=1, device_id={"wide": lax.rem(w + t, wide)}, device_id_type=MESH
        )
    pl.semaphore_wait(barrier, narrow + wide - 2)

    sends = []

    def push(src, dst, send_sem, recv_sem, target):
        copy = pltpu.make_async_remote_copy(
            src_ref=src, dst_ref=dst, send_sem=send_sem, recv_sem=recv_sem,
            device_id=target, device_id_type=MESH,
        )
        copy.start()
        sends.append(copy)

    def arrived(dst, recv_sem, send_sem, target):
        pltpu.make_async_remote_copy(
            src_ref=dst, dst_ref=dst, send_sem=send_sem, recv_sem=recv_sem,
            device_id=target, device_id_type=MESH,
        ).wait_recv()

    for peer in narrow_peers:
        push(coef.at[peer], recv_a.at[m], a_send.at[peer], a_recv.at[m], {"narrow": peer})
    own.wait()
    loads[0].wait()
    for peer in narrow_peers:
        arrived(recv_a.at[peer], a_recv.at[peer], a_send.at[peer], {"narrow": peer})

    plane = dot(recv_a[...].reshape(-1, LANES), order[...]).astype(BF16)

    def send_points(d):
        send_b[d] = dot(zt[d], plane).astype(BF16)
        push(send_b.at[d], recv_b.at[w], b_send.at[d], b_recv.at[w], {"wide": d})

    for t in far_first:
        send_points(2 * pair_of[t])
        send_points(2 * pair_of[t] + 1)
    send_points(beside)
    for load in loads[2:]:
        load.start()
    recv_b[w] = dot(zt[w], plane).astype(BF16)

    lane = lax.broadcasted_iota(jnp.int32, (1, LANES), 1)
    even = lax.rem(lane, 2) == 0

    low = lane < LANES // 2
    local = 2 * lax.div(lax.rem(lane, LANES // 2), 2) + lax.div(lane, LANES // 2)

    def slope_of(field, first):
        rate = (local + first).astype(F32) * (2.0 * math.pi / gx_size)
        after = pltpu.roll(field, LANES - 1, 1)
        before = pltpu.roll(field, 1, 1)
        return jnp.where(even, rate * after, -rate * before)

    def stacked(pair):
        fields = []
        for s in (0, 1):
            block = recv_b[2 * pair + s].astype(F32)
            val, dz = block[:rows], block[rows:]
            dx = slope_of(val, (2 * pair + s) * (LANES // 2))
            fields.append(jnp.concatenate([val, dx, dz], axis=0))
        return split(*fields)

    def split(first, second):
        turned = [pltpu.roll(field, LANES // 2, 1) for field in (first, second)]
        return (
            jnp.where(low, first, turned[1]).astype(BF16),
            jnp.where(low, turned[0], second).astype(BF16),
        )

    quads = pairs // 2
    quad_of = [lax.div(pair_of[2 * u], 2) for u in range(quads)]
    middle = gx_size // 2
    tile = 256
    cuts = [slice(c, c + tile) for c in range(0, middle, tile)]
    for u in range(quads):
        quad = quad_of[u]
        for t in (2 * u, 2 * u + 1):
            for d in (2 * pair_of[t], 2 * pair_of[t] + 1) if t else (beside,):
                arrived(recv_b.at[d], b_recv.at[d], b_send.at[d], {"wide": d})
        both = [stacked(2 * quad), stacked(2 * quad + 1)]
        fields = [jnp.concatenate([half[i] for half in both], axis=1) for i in (0, 1)]
        if u == 0:
            loads[1].wait()
        if u == quads - 1:
            loads[2].wait()
            loads[3].wait()
        for cut in cuts:
            parts = [dot(fields[i], bt[quad, i, :, cut]) for i in (0, 1)]
            if u > 0:
                parts = [parts[i] + acc[i, :, cut] for i in (0, 1)]
            if u < quads - 1:
                for i in (0, 1):
                    acc[i, :, cut] = parts[i]
            else:
                totals = []
                for part, start in ((parts[0] + parts[1], 0), (parts[0] - parts[1], middle)):
                    at = slice(cut.start + start, cut.stop + start)
                    buoy[0, :, at] = part[:rows].astype(BF16)
                    total = speed[0, 0, :, at].astype(F32) * part[rows : 2 * rows]
                    total = total + speed[1, 0, :, at].astype(F32) * dy[0, :, at].astype(F32)
                    totals.append(total + speed[2, 0, :, at].astype(F32) * part[2 * rows :])
                adv[0, :, cut] = (-(totals[0] + totals[1])).astype(BF16)
                adv[1, :, cut] = (totals[1] - totals[0]).astype(BF16)
    grid_copy = pltpu.make_async_copy(buoy, grid_out, local_sem.at[6])
    grid_copy.start()

    for u in reversed(range(quads)):
        quad = quad_of[u]
        halves = [dot_last(adv[i], bt[quad, i]) for i in (0, 1)]
        for s in (0, 1):
            columns = slice(s * LANES, (s + 1) * LANES)
            first, second = split(halves[0][:, columns], halves[1][:, columns])
            send_e[4 * quad + 2 * s] = first
            send_e[4 * quad + 2 * s + 1] = second
        for t in (2 * u + 1, 2 * u):
            for d in (2 * pair_of[t], 2 * pair_of[t] + 1) if t else (beside,):
                push(send_e.at[d], recv_e.at[w], e_send.at[d], e_recv.at[w], {"wide": d})
    points[w] = dot(send_e[w], order_back[...]).astype(BF16)
    loads[4].wait()
    for t in range(pairs):
        for d in (2 * pair_of[t], 2 * pair_of[t] + 1) if t else (beside,):
            arrived(recv_e.at[d], e_recv.at[d], e_send.at[d], {"wide": d})
            points[d] = dot(recv_e[d], order_back[...]).astype(BF16)

    all_points = points[...].reshape(-1, LANES)
    for peer in narrow_peers:
        send_f[peer] = dot(vt[peer], all_points).astype(BF16)
        push(send_f.at[peer], advect_out.at[m], f_send.at[peer], f_recv.at[m], {"narrow": peer})
    send_f[m] = dot(vt[m], all_points).astype(BF16)
    kept = pltpu.make_async_copy(send_f.at[m], advect_out.at[m], local_sem.at[7])
    kept.start()
    for peer in narrow_peers:
        arrived(advect_out.at[peer], f_recv.at[peer], f_send.at[peer], {"narrow": peer})
    kept.wait()
    grid_copy.wait()
    for copy in sends:
        copy.wait_send()


def hand_over(advect, grid, advect_out, grid_out, advect_held, grid_held, sem):
    routes = [(advect, advect_held, advect_out), (grid, grid_held, grid_out)]
    fetches = [
        pltpu.make_async_copy(src, held, sem.at[i]) for i, (src, held, _) in enumerate(routes)
    ]
    stores = [
        pltpu.make_async_copy(held, dst, sem.at[2 + i]) for i, (_, held, dst) in enumerate(routes)
    ]
    for fetch in fetches:
        fetch.start()
    for fetch, store in zip(fetches, stores):
        fetch.wait()
        store.start()
    for store in stores:
        store.wait()


def by_kernel(wide, narrow, coef, velocity, slope_y):
    degrees = coef.shape[1]
    rows, gx_size = slope_y.shape[1:]
    kz_size, kx_size, gz_size = degrees * narrow, LANES * wide, rows * wide
    pairs = wide // 2
    values, slopes = z_tables(gz_size, kz_size)
    basis = x_table(gx_size, kx_size)
    zt = np.concatenate(
        [values.reshape(wide, rows, kz_size), slopes.reshape(wide, rows, kz_size)], axis=1
    )
    order_of = np.arange(LANES).reshape(-1, 2, 2).transpose(1, 0, 2).reshape(-1)
    order = np.zeros((LANES, LANES), ml_dtypes.bfloat16)
    order[order_of, np.arange(LANES)] = 1
    order_back = np.ascontiguousarray(order.T)
    bt = np.ascontiguousarray(
        basis[: gx_size // 2].T.reshape(pairs // 2, 4 * LANES // 4, 2, 2, gx_size // 2)
        .transpose(0, 2, 1, 3, 4).reshape(pairs // 2, 2, 2 * LANES, gx_size // 2)
    )
    vt = np.ascontiguousarray(values.T).reshape(narrow, degrees, gz_size)
    hbm = pl.BlockSpec(memory_space=pltpu.HBM)
    dma = pltpu.SemaphoreType.DMA
    advect, grid = pl.pallas_call(
        functools.partial(kernel, wide, narrow, rows, gx_size),
        out_shape=(
            jax.ShapeDtypeStruct(coef.shape, BF16),
            jax.ShapeDtypeStruct(slope_y.shape, BF16),
        ),
        in_specs=[hbm] * 3 + [pl.BlockSpec(memory_space=pltpu.VMEM)] * 2 + [hbm] * 3,
        out_specs=(hbm, hbm),
        scratch_shapes=[
            pltpu.VMEM(zt.shape, BF16),
            pltpu.VMEM(bt.shape, BF16),
            pltpu.VMEM(vt.shape, BF16),
            pltpu.VMEM(velocity.shape, BF16),
            pltpu.VMEM(slope_y.shape, BF16),
            pltpu.VMEM((narrow, degrees, LANES), BF16),
            pltpu.VMEM((wide, 2 * rows, LANES), BF16),
            pltpu.VMEM((wide, 2 * rows, LANES), BF16),
            pltpu.VMEM((2, 3 * rows, gx_size // 2), F32),
            pltpu.VMEM((2, rows, gx_size // 2), BF16),
            pltpu.VMEM(slope_y.shape, BF16),
            pltpu.VMEM((wide, rows, LANES), BF16),
            pltpu.VMEM((wide, rows, LANES), BF16),
            pltpu.VMEM((wide, rows, LANES), BF16),
            pltpu.VMEM((narrow, degrees, LANES), BF16),
            dma((8,)),
            dma((narrow,)),
            dma((narrow,)),
            dma((wide,)),
            dma((wide,)),
            dma((wide,)),
            dma((wide,)),
            dma((narrow,)),
            dma((narrow,)),
        ],
        compiler_params=pltpu.CompilerParams(
            collective_id=0, has_side_effects=True, vmem_limit_bytes=VMEM_BYTES
        ),
    )(coef, velocity, slope_y, order, order_back, zt, bt, vt)
    return pl.pallas_call(
        hand_over,
        out_shape=(
            jax.ShapeDtypeStruct(coef.shape, BF16),
            jax.ShapeDtypeStruct(slope_y.shape, BF16),
        ),
        in_specs=[hbm] * 2,
        out_specs=(hbm, hbm),
        scratch_shapes=[
            pltpu.VMEM(coef.shape, BF16),
            pltpu.VMEM(slope_y.shape, BF16),
            dma((4,)),
        ],
        compiler_params=pltpu.CompilerParams(vmem_limit_bytes=VMEM_BYTES),
    )(advect, grid)


def x_slope(wave_in, gx_size):
    width_now = wave_in.shape[-1]
    paired = wave_in.astype(F32).reshape(wave_in.shape[:-1] + (width_now // 2, 2))
    harmonic = lax.iota(jnp.int32, width_now // 2).astype(F32)
    omega_rate = harmonic * (2.0 * math.pi / gx_size)
    cos_part = omega_rate * paired[..., 1]
    sin_part = -omega_rate * paired[..., 0]
    return jnp.stack([cos_part, sin_part], axis=-1).reshape(wave_in.shape).astype(BF16)


def by_collectives(wide, narrow, coef, velocity, slope_y):
    gz_size, gx_size = slope_y.shape[1] * wide, slope_y.shape[2]
    kz_size, kx_size = coef.shape[1] * narrow, coef.shape[2] * wide
    values, slopes = z_tables(gz_size, kz_size)
    basis = x_table(gx_size, kx_size)
    einsum = functools.partial(jnp.einsum, preferred_element_type=F32)
    swap = functools.partial(lax.all_to_all, tiled=True)
    plane = swap(coef, "narrow", split_axis=0, concat_axis=1)
    wave_val = einsum("jn,ynk->yjk", values, plane).astype(BF16)
    wave_dz = einsum("jn,ynk->yjk", slopes, plane).astype(BF16)
    wave_val = swap(wave_val, "wide", split_axis=1, concat_axis=2)
    wave_dz = swap(wave_dz, "wide", split_axis=1, concat_axis=2)
    grid_val, grid_dx, grid_dz = (
        einsum("yjk,gk->yjg", field, basis)
        for field in (wave_val, x_slope(wave_val, gx_size), wave_dz)
    )
    total = velocity[0] * grid_dx + velocity[1] * slope_y.astype(F32) + velocity[2] * grid_dz
    half_coef = einsum("yjg,gk->yjk", (-total).astype(BF16), basis).astype(BF16)
    half_coef = swap(half_coef, "wide", split_axis=2, concat_axis=1)
    coef_z = einsum("jn,yjk->ynk", values, half_coef).astype(BF16)
    advect = swap(coef_z, "narrow", split_axis=1, concat_axis=0)
    return advect, grid_val.astype(BF16)


def solution(mesh):
    wide, narrow = mesh.shape["wide"], mesh.shape["narrow"]

    def on_device(coef, velocity, slope_y):
        whole_tiles = (
            slope_y.shape[0] == 1
            and coef.shape[1] % 16 == 0
            and coef.shape[2] == LANES
            and slope_y.shape[1] % 16 == 0
            and slope_y.shape[2] % 512 == 0
            and wide >= 4
            and wide & (wide - 1) == 0
        )
        plan = by_kernel if whole_tiles else by_collectives
        return plan(wide, narrow, coef, velocity, slope_y)

    return jax.shard_map(
        on_device,
        mesh=mesh,
        in_specs=(
            P(None, "narrow", "wide"),
            P(None, "narrow", "wide", None),
            P("narrow", "wide", None),
        ),
        out_specs=(P(None, "narrow", "wide"), P("narrow", "wide", None)),
        check_vma=False,
    )
```

```python
import functools
import math

import jax
import jax.numpy as jnp
import ml_dtypes
import numpy as np
from jax import lax
from jax.experimental import pallas as pl
from jax.experimental.pallas import tpu as pltpu
from jax.sharding import PartitionSpec as P

MESH = pl.DeviceIdType.MESH
F32 = jnp.float32
BF16 = jnp.bfloat16
LANES = 128
VMEM_BYTES = 64 * 1024 * 1024 - 256 * 1024


def x_table(gx_size, kx_size):
    points = np.arange(gx_size, dtype=np.int32)[:, None]
    column_id = np.arange(kx_size, dtype=np.int32)[None, :]
    harmonic = column_id // 2
    angles = (harmonic * points % gx_size).astype(np.float32) * np.float32(2.0 * math.pi / gx_size)
    weights = np.where(
        harmonic == 0, math.sqrt(1.0 / gx_size), math.sqrt(2.0 / gx_size)
    ).astype(np.float32)
    raw = np.where(column_id % 2 == 0, np.cos(angles), np.sin(angles))
    return (raw * weights).astype(ml_dtypes.bfloat16)


def z_tables(gz_size, kz_size):
    nodes = np.arange(gz_size, dtype=np.int32)[:, None]
    degree = np.arange(kz_size, dtype=np.int32)[None, :]
    step = np.float32(math.pi / (2.0 * gz_size))
    angles = (degree * (2 * nodes + 1) % (4 * gz_size)).astype(np.float32) * step
    polar = (2 * nodes + 1).astype(np.float32) * step
    weights = np.where(
        degree == 0, math.sqrt(1.0 / gz_size), math.sqrt(2.0 / gz_size)
    ).astype(np.float32)
    values = weights * np.cos(angles)
    slopes = weights * np.float32(2.0 / gz_size) * degree.astype(np.float32)
    slopes = slopes * np.sin(angles) / np.sin(polar)
    return values.astype(ml_dtypes.bfloat16), slopes.astype(ml_dtypes.bfloat16)


def dot(left, right):
    return jnp.dot(left, right, preferred_element_type=F32)


def dot_last(left, right):
    return lax.dot_general(left, right, (((1,), (1,)), ((), ())), preferred_element_type=F32)


def flip_bits(index, mask, size):
    total, bit = 0, 1
    while bit < size:
        digit = lax.rem(lax.div(index, bit), 2)
        total = total + bit * (1 - digit if mask & bit else digit)
        bit *= 2
    return total


def kernel(
    wide, narrow, groups, gx_size,
    coef, velocity, slope_y, zt_hbm, bt_hbm, vt_hbm,
    advect_out, grid_out,
    zt, bt, vt, speed, dy,
    recv_a, send_b, recv_b, acc, adv, buoy, send_e, recv_e, send_f,
    local_sem, a_send, a_recv, b_send, b_recv, e_send, e_recv, f_send, f_recv,
):
    pairs = wide // 2
    w = lax.axis_index("wide")
    m = lax.axis_index("narrow")
    mine = lax.div(w, 2)
    beside = 2 * mine + 1 - lax.rem(w, 2)
    narrow_peers = [lax.rem(m + r, narrow) for r in range(1, narrow)]
    pair_of = [flip_bits(mine, t, pairs) for t in range(pairs)]
    far_first = list(range(pairs - 1, 0, -1))

    def others(t):
        return (2 * pair_of[t], 2 * pair_of[t] + 1) if t else (beside,)

    own = pltpu.make_async_copy(coef.at[m], recv_a.at[m], local_sem.at[0])
    own.start()
    loads = [
        pltpu.make_async_copy(src, dst, local_sem.at[1 + i])
        for i, (src, dst) in enumerate(
            [(zt_hbm, zt), (bt_hbm, bt), (velocity, speed), (slope_y, dy), (vt_hbm, vt)]
        )
    ]
    for load in loads[:2]:
        load.start()

    barrier = pltpu.get_barrier_semaphore()
    for peer in narrow_peers:
        pl.semaphore_signal(barrier, inc=1, device_id={"narrow": peer}, device_id_type=MESH)
    for t in range(1, wide):
        pl.semaphore_signal(
            barrier, inc=1, device_id={"wide": lax.rem(w + t, wide)}, device_id_type=MESH
        )
    pl.semaphore_wait(barrier, narrow + wide - 2)

    sends = []

    def push(src, dst, send_sem, recv_sem, target):
        copy = pltpu.make_async_remote_copy(
            src_ref=src, dst_ref=dst, send_sem=send_sem, recv_sem=recv_sem,
            device_id=target, device_id_type=MESH,
        )
        copy.start()
        sends.append(copy)

    def arrived(dst, recv_sem, send_sem, target):
        pltpu.make_async_remote_copy(
            src_ref=dst, dst_ref=dst, send_sem=send_sem, recv_sem=recv_sem,
            device_id=target, device_id_type=MESH,
        ).wait_recv()

    for peer in narrow_peers:
        push(coef.at[peer], recv_a.at[m], a_send.at[peer], a_recv.at[m], {"narrow": peer})
    own.wait()
    loads[0].wait()
    for peer in narrow_peers:
        arrived(recv_a.at[peer], a_recv.at[peer], a_send.at[peer], {"narrow": peer})

    plane = recv_a[...].reshape(-1, LANES)

    def of_group(g):
        return pl.ds(2 * groups[g][0], 2 * groups[g][1])

    def points_at(d, g):
        return dot(zt[d, of_group(g)], plane).astype(BF16)

    def send_points(g, d):
        push(
            send_b.at[d, of_group(g)], recv_b.at[w, of_group(g)],
            b_send.at[g, d], b_recv.at[g, w], {"wide": d},
        )

    for g in range(len(groups)):
        for t in far_first + [0]:
            for d in others(t):
                send_b[d, of_group(g)] = points_at(d, g)
                if g == 0:
                    send_points(g, d)
        recv_b[w, of_group(g)] = points_at(w, g)
    for load in loads[2:]:
        load.start()

    lane = lax.broadcasted_iota(jnp.int32, (1, LANES), 1)
    even = lax.rem(lane, 2) == 0

    def slope_of(field, first):
        harmonic = (lax.div(lane, 2) + first).astype(F32)
        rate = harmonic * (2.0 * math.pi / gx_size)
        wide_field = field.astype(F32)
        after = pltpu.roll(wide_field, LANES - 1, 1)
        before = pltpu.roll(wide_field, 1, 1)
        return jnp.where(even, rate * after, -rate * before).astype(BF16)

    def stacked(pair, g):
        count = groups[g][1]
        fields = []
        for s in (0, 1):
            block = recv_b[2 * pair + s, of_group(g)]
            val, dz = block[:count], block[count:]
            dx = slope_of(val, (2 * pair + s) * (LANES // 2))
            fields.append(jnp.concatenate([val, dx, dz], axis=0))
        return jnp.concatenate(fields, axis=1)

    tile = 512
    cuts = [slice(c, c + tile) for c in range(0, gx_size, tile)]
    for g, (first, count) in enumerate(groups):
        rows = slice(first, first + count)
        for t in range(pairs):
            pair = pair_of[t]
            if g == 0 and t == pairs // 2:
                while sends:
                    sends.pop(0).wait_send()
                for later in range(1, len(groups)):
                    for peer in [d for u in far_first + [0] for d in others(u)]:
                        send_points(later, peer)
            for d in others(t):
                arrived(
                    recv_b.at[d, of_group(g)], b_recv.at[g, d], b_send.at[g, d], {"wide": d}
                )
            fields = stacked(pair, g)
            if g == 0 and t == 0:
                loads[1].wait()
            if g == 0 and t == pairs - 1:
                loads[2].wait()
                loads[3].wait()
            for cut in cuts:
                part = dot(fields, bt[pair, :, cut])
                if t > 0:
                    part = part + acc[: 3 * count, cut]
                if t < pairs - 1:
                    acc[: 3 * count, cut] = part
                else:
                    buoy[0, rows, cut] = part[:count].astype(BF16)
                    total = speed[0, 0, rows, cut].astype(F32) * part[count : 2 * count]
                    total = total + speed[1, 0, rows, cut].astype(F32) * dy[0, rows, cut].astype(F32)
                    total = total + speed[2, 0, rows, cut].astype(F32) * part[2 * count :]
                    adv[rows, cut] = (-total).astype(BF16)

        for t in far_first + [0]:
            pair = pair_of[t]
            half = dot_last(adv[rows], bt[pair]).astype(BF16)
            for s in (0, 1):
                send_e[2 * pair + s, rows] = half[:, s * LANES : (s + 1) * LANES]
            for d in others(t):
                push(
                    send_e.at[d, pl.ds(first, count)], recv_e.at[w, pl.ds(first, count)],
                    e_send.at[g, d], e_recv.at[g, w], {"wide": d},
                )
    grid_copy = pltpu.make_async_copy(buoy, grid_out, local_sem.at[6])
    grid_copy.start()
    recv_e[w] = send_e[w]
    loads[4].wait()
    for g, (first, count) in enumerate(groups):
        for t in range(pairs):
            for d in others(t):
                arrived(
                    recv_e.at[d, pl.ds(first, count)], e_recv.at[g, d], e_send.at[g, d],
                    {"wide": d},
                )

    points = recv_e[...].reshape(-1, LANES)
    for peer in narrow_peers:
        send_f[peer] = dot(vt[peer], points).astype(BF16)
        push(send_f.at[peer], advect_out.at[m], f_send.at[peer], f_recv.at[m], {"narrow": peer})
    send_f[m] = dot(vt[m], points).astype(BF16)
    kept = pltpu.make_async_copy(send_f.at[m], advect_out.at[m], local_sem.at[7])
    kept.start()
    for peer in narrow_peers:
        arrived(advect_out.at[peer], f_recv.at[peer], f_send.at[peer], {"narrow": peer})
    kept.wait()
    grid_copy.wait()
    for copy in sends:
        copy.wait_send()


def hand_over(advect, grid, advect_out, grid_out, advect_held, grid_held, sem):
    routes = [(advect, advect_held, advect_out), (grid, grid_held, grid_out)]
    fetches = [
        pltpu.make_async_copy(src, held, sem.at[i]) for i, (src, held, _) in enumerate(routes)
    ]
    stores = [
        pltpu.make_async_copy(held, dst, sem.at[2 + i]) for i, (_, held, dst) in enumerate(routes)
    ]
    for fetch in fetches:
        fetch.start()
    for fetch, store in zip(fetches, stores):
        fetch.wait()
        store.start()
    for store in stores:
        store.wait()


def by_kernel(wide, narrow, coef, velocity, slope_y):
    degrees = coef.shape[1]
    rows, gx_size = slope_y.shape[1:]
    kz_size, kx_size, gz_size = degrees * narrow, LANES * wide, rows * wide
    pairs = wide // 2
    values, slopes = z_tables(gz_size, kz_size)
    basis = x_table(gx_size, kx_size)
    early = max(16, rows * 2 // 3 // 16 * 16)
    groups = [(0, early), (early, rows - early)] if early < rows else [(0, rows)]
    values_at = values.reshape(wide, rows, kz_size)
    slopes_at = slopes.reshape(wide, rows, kz_size)
    zt = np.concatenate(
        [
            table[:, first : first + count]
            for first, count in groups
            for table in (values_at, slopes_at)
        ],
        axis=1,
    )
    bt = np.ascontiguousarray(basis.T).reshape(pairs, 2 * LANES, gx_size)
    vt = np.ascontiguousarray(values.T).reshape(narrow, degrees, gz_size)
    hbm = pl.BlockSpec(memory_space=pltpu.HBM)
    dma = pltpu.SemaphoreType.DMA
    advect, grid = pl.pallas_call(
        functools.partial(kernel, wide, narrow, groups, gx_size),
        out_shape=(
            jax.ShapeDtypeStruct(coef.shape, BF16),
            jax.ShapeDtypeStruct(slope_y.shape, BF16),
        ),
        in_specs=[hbm] * 6,
        out_specs=(hbm, hbm),
        scratch_shapes=[
            pltpu.VMEM(zt.shape, BF16),
            pltpu.VMEM(bt.shape, BF16),
            pltpu.VMEM(vt.shape, BF16),
            pltpu.VMEM(velocity.shape, BF16),
            pltpu.VMEM(slope_y.shape, BF16),
            pltpu.VMEM((narrow, degrees, LANES), BF16),
            pltpu.VMEM((wide, 2 * rows, LANES), BF16),
            pltpu.VMEM((wide, 2 * rows, LANES), BF16),
            pltpu.VMEM((3 * groups[0][1], gx_size), F32),
            pltpu.VMEM((rows, gx_size), BF16),
            pltpu.VMEM(slope_y.shape, BF16),
            pltpu.VMEM((wide, rows, LANES), BF16),
            pltpu.VMEM((wide, rows, LANES), BF16),
            pltpu.VMEM((narrow, degrees, LANES), BF16),
            dma((8,)),
            dma((narrow,)),
            dma((narrow,)),
            dma((len(groups), wide)),
            dma((len(groups), wide)),
            dma((len(groups), wide)),
            dma((len(groups), wide)),
            dma((narrow,)),
            dma((narrow,)),
        ],
        compiler_params=pltpu.CompilerParams(
            collective_id=0, has_side_effects=True, vmem_limit_bytes=VMEM_BYTES
        ),
    )(coef, velocity, slope_y, zt, bt, vt)
    return pl.pallas_call(
        hand_over,
        out_shape=(
            jax.ShapeDtypeStruct(coef.shape, BF16),
            jax.ShapeDtypeStruct(slope_y.shape, BF16),
        ),
        in_specs=[hbm] * 2,
        out_specs=(hbm, hbm),
        scratch_shapes=[
            pltpu.VMEM(coef.shape, BF16),
            pltpu.VMEM(slope_y.shape, BF16),
            dma((4,)),
        ],
        compiler_params=pltpu.CompilerParams(vmem_limit_bytes=VMEM_BYTES),
    )(advect, grid)


def x_slope(wave_in, gx_size):
    width_now = wave_in.shape[-1]
    paired = wave_in.astype(F32).reshape(wave_in.shape[:-1] + (width_now // 2, 2))
    harmonic = lax.iota(jnp.int32, width_now // 2).astype(F32)
    omega_rate = harmonic * (2.0 * math.pi / gx_size)
    cos_part = omega_rate * paired[..., 1]
    sin_part = -omega_rate * paired[..., 0]
    return jnp.stack([cos_part, sin_part], axis=-1).reshape(wave_in.shape).astype(BF16)


def by_collectives(wide, narrow, coef, velocity, slope_y):
    gz_size, gx_size = slope_y.shape[1] * wide, slope_y.shape[2]
    kz_size, kx_size = coef.shape[1] * narrow, coef.shape[2] * wide
    values, slopes = z_tables(gz_size, kz_size)
    basis = x_table(gx_size, kx_size)
    einsum = functools.partial(jnp.einsum, preferred_element_type=F32)
    swap = functools.partial(lax.all_to_all, tiled=True)
    plane = swap(coef, "narrow", split_axis=0, concat_axis=1)
    wave_val = einsum("jn,ynk->yjk", values, plane).astype(BF16)
    wave_dz = einsum("jn,ynk->yjk", slopes, plane).astype(BF16)
    wave_val = swap(wave_val, "wide", split_axis=1, concat_axis=2)
    wave_dz = swap(wave_dz, "wide", split_axis=1, concat_axis=2)
    grid_val, grid_dx, grid_dz = (
        einsum("yjk,gk->yjg", field, basis)
        for field in (wave_val, x_slope(wave_val, gx_size), wave_dz)
    )
    total = velocity[0] * grid_dx + velocity[1] * slope_y.astype(F32) + velocity[2] * grid_dz
    half_coef = einsum("yjg,gk->yjk", (-total).astype(BF16), basis).astype(BF16)
    half_coef = swap(half_coef, "wide", split_axis=2, concat_axis=1)
    coef_z = einsum("jn,yjk->ynk", values, half_coef).astype(BF16)
    advect = swap(coef_z, "narrow", split_axis=1, concat_axis=0)
    return advect, grid_val.astype(BF16)


def solution(mesh):
    wide, narrow = mesh.shape["wide"], mesh.shape["narrow"]

    def on_device(coef, velocity, slope_y):
        whole_tiles = (
            slope_y.shape[0] == 1
            and coef.shape[1] % 16 == 0
            and coef.shape[2] == LANES
            and slope_y.shape[1] % 16 == 0
            and slope_y.shape[2] % 512 == 0
            and wide >= 4
            and wide & (wide - 1) == 0
        )
        plan = by_kernel if whole_tiles else by_collectives
        return plan(wide, narrow, coef, velocity, slope_y)

    return jax.shard_map(
        on_device,
        mesh=mesh,
        in_specs=(
            P(None, "narrow", "wide"),
            P(None, "narrow", "wide", None),
            P("narrow", "wide", None),
        ),
        out_specs=(P(None, "narrow", "wide"), P("narrow", "wide", None)),
        check_vma=False,
    )
```

```python
import functools
import math

import jax
import jax.numpy as jnp
import ml_dtypes
import numpy as np
from jax import lax
from jax.experimental import pallas as pl
from jax.experimental.pallas import tpu as pltpu
from jax.sharding import PartitionSpec as P

MESH = pl.DeviceIdType.MESH
F32 = jnp.float32
BF16 = jnp.bfloat16
LANES = 128
VMEM_BYTES = 64 * 1024 * 1024 - 640 * 1024


def x_table(gx_size, kx_size):
    points = np.arange(gx_size, dtype=np.int32)[:, None]
    column_id = np.arange(kx_size, dtype=np.int32)[None, :]
    harmonic = column_id // 2
    angles = (harmonic * points % gx_size).astype(np.float32) * np.float32(2.0 * math.pi / gx_size)
    weights = np.where(
        harmonic == 0, math.sqrt(1.0 / gx_size), math.sqrt(2.0 / gx_size)
    ).astype(np.float32)
    raw = np.where(column_id % 2 == 0, np.cos(angles), np.sin(angles))
    return (raw * weights).astype(ml_dtypes.bfloat16)


def z_tables(gz_size, kz_size):
    nodes = np.arange(gz_size, dtype=np.int32)[:, None]
    degree = np.arange(kz_size, dtype=np.int32)[None, :]
    step = np.float32(math.pi / (2.0 * gz_size))
    angles = (degree * (2 * nodes + 1) % (4 * gz_size)).astype(np.float32) * step
    polar = (2 * nodes + 1).astype(np.float32) * step
    weights = np.where(
        degree == 0, math.sqrt(1.0 / gz_size), math.sqrt(2.0 / gz_size)
    ).astype(np.float32)
    values = weights * np.cos(angles)
    slopes = weights * np.float32(2.0 / gz_size) * degree.astype(np.float32)
    slopes = slopes * np.sin(angles) / np.sin(polar)
    return values.astype(ml_dtypes.bfloat16), slopes.astype(ml_dtypes.bfloat16)


def dot(left, right):
    return jnp.dot(left, right, preferred_element_type=F32)


def dot_last(left, right):
    return lax.dot_general(left, right, (((1,), (1,)), ((), ())), preferred_element_type=F32)


def flip_bits(index, mask, size):
    total, bit = 0, 1
    while bit < size:
        digit = lax.rem(lax.div(index, bit), 2)
        total = total + bit * (1 - digit if mask & bit else digit)
        bit *= 2
    return total


def kernel(
    wide, narrow, rows, gx_size,
    coef, velocity, slope_y, zt_hbm, bt_hbm, vt_hbm,
    advect_out, grid_out,
    zt, bt, vt, speed, dy,
    recv_a, send_b, recv_b, acc, adv, buoy, send_e, recv_e, send_f,
    local_sem, a_send, a_recv, b_send, b_recv, e_send, e_recv, f_send, f_recv,
):
    pairs = wide // 2
    w = lax.axis_index("wide")
    m = lax.axis_index("narrow")
    mine = lax.div(w, 2)
    beside = 2 * mine + 1 - lax.rem(w, 2)
    narrow_peers = [lax.rem(m + r, narrow) for r in range(1, narrow)]
    pair_of = [flip_bits(mine, t, pairs) for t in range(pairs)]
    far_first = list(range(pairs - 1, 0, -1))

    own = pltpu.make_async_copy(coef.at[m], recv_a.at[m], local_sem.at[0])
    own.start()
    loads = [
        pltpu.make_async_copy(src, dst, local_sem.at[1 + i])
        for i, (src, dst) in enumerate(
            [(zt_hbm, zt), (bt_hbm, bt), (velocity, speed), (slope_y, dy), (vt_hbm, vt)]
        )
    ]
    for load in loads[:2]:
        load.start()

    barrier = pltpu.get_barrier_semaphore()
    for peer in narrow_peers:
        pl.semaphore_signal(barrier, inc=1, device_id={"narrow": peer}, device_id_type=MESH)
    for t in range(1, wide):
        pl.semaphore_signal(
            barrier, inc=1, device_id={"wide": lax.rem(w + t, wide)}, device_id_type=MESH
        )
    pl.semaphore_wait(barrier, narrow + wide - 2)

    sends = []

    def push(src, dst, send_sem, recv_sem, target):
        copy = pltpu.make_async_remote_copy(
            src_ref=src, dst_ref=dst, send_sem=send_sem, recv_sem=recv_sem,
            device_id=target, device_id_type=MESH,
        )
        copy.start()
        sends.append(copy)

    def arrived(dst, recv_sem, send_sem, target):
        pltpu.make_async_remote_copy(
            src_ref=dst, dst_ref=dst, send_sem=send_sem, recv_sem=recv_sem,
            device_id=target, device_id_type=MESH,
        ).wait_recv()

    for peer in narrow_peers:
        push(coef.at[peer], recv_a.at[m], a_send.at[peer], a_recv.at[m], {"narrow": peer})
    own.wait()
    loads[0].wait()
    for peer in narrow_peers:
        arrived(recv_a.at[peer], a_recv.at[peer], a_send.at[peer], {"narrow": peer})

    plane = recv_a[...].reshape(-1, LANES)

    def send_points(d):
        send_b[d] = dot(zt[d], plane).astype(BF16)
        push(send_b.at[d], recv_b.at[w], b_send.at[d], b_recv.at[w], {"wide": d})

    for t in far_first:
        send_points(2 * pair_of[t])
        send_points(2 * pair_of[t] + 1)
    send_points(beside)
    for load in loads[2:]:
        load.start()
    recv_b[w] = dot(zt[w], plane).astype(BF16)

    lane = lax.broadcasted_iota(jnp.int32, (1, LANES), 1)
    even = lax.rem(lane, 2) == 0

    def slope_of(field, first):
        harmonic = (lax.div(lane, 2) + first).astype(F32)
        rate = harmonic * (2.0 * math.pi / gx_size)
        wide_field = field.astype(F32)
        after = pltpu.roll(wide_field, LANES - 1, 1)
        before = pltpu.roll(wide_field, 1, 1)
        return jnp.where(even, rate * after, -rate * before).astype(BF16)

    def stacked(pair):
        fields = []
        for s in (0, 1):
            block = recv_b[2 * pair + s]
            val, dz = block[:rows], block[rows:]
            dx = slope_of(val, (2 * pair + s) * (LANES // 2))
            fields.append(jnp.concatenate([val, dx, dz], axis=0))
        return jnp.concatenate(fields, axis=1)

    tile = 512
    cuts = [slice(c, c + tile) for c in range(0, gx_size, tile)]
    for t in range(pairs):
        pair = pair_of[t]
        if t == 0:
            arrived(recv_b.at[beside], b_recv.at[beside], b_send.at[beside], {"wide": beside})
            loads[1].wait()
        else:
            for d in (2 * pair, 2 * pair + 1):
                arrived(recv_b.at[d], b_recv.at[d], b_send.at[d], {"wide": d})
        fields = stacked(pair)
        if t == pairs - 1:
            loads[2].wait()
            loads[3].wait()
        for cut in cuts:
            part = dot(fields, bt[pair, :, cut])
            if t > 0:
                part = part + acc[:, cut]
            if t < pairs - 1:
                acc[:, cut] = part
            else:
                buoy[0, :, cut] = part[:rows].astype(BF16)
                total = speed[0, 0, :, cut].astype(F32) * part[rows : 2 * rows]
                total = total + speed[1, 0, :, cut].astype(F32) * dy[0, :, cut].astype(F32)
                total = total + speed[2, 0, :, cut].astype(F32) * part[2 * rows :]
                adv[:, cut] = (-total).astype(BF16)
    grid_copy = pltpu.make_async_copy(buoy, grid_out, local_sem.at[6])
    grid_copy.start()

    for t in far_first + [0]:
        pair = pair_of[t]
        half = dot_last(adv[...], bt[pair]).astype(BF16)
        for s in (0, 1):
            send_e[2 * pair + s] = half[:, s * LANES : (s + 1) * LANES]
        for d in (2 * pair, 2 * pair + 1) if t else (beside,):
            push(send_e.at[d], recv_e.at[w], e_send.at[d], e_recv.at[w], {"wide": d})
    recv_e[w] = send_e[w]
    loads[4].wait()
    for t in range(pairs):
        for d in (2 * pair_of[t], 2 * pair_of[t] + 1) if t else (beside,):
            arrived(recv_e.at[d], e_recv.at[d], e_send.at[d], {"wide": d})

    points = recv_e[...].reshape(-1, LANES)
    for peer in narrow_peers:
        send_f[peer] = dot(vt[peer], points).astype(BF16)
        push(send_f.at[peer], advect_out.at[m], f_send.at[peer], f_recv.at[m], {"narrow": peer})
    send_f[m] = dot(vt[m], points).astype(BF16)
    kept = pltpu.make_async_copy(send_f.at[m], advect_out.at[m], local_sem.at[7])
    kept.start()
    for peer in narrow_peers:
        arrived(advect_out.at[peer], f_recv.at[peer], f_send.at[peer], {"narrow": peer})
    kept.wait()
    grid_copy.wait()
    for copy in sends:
        copy.wait_send()


def by_kernel(wide, narrow, coef, velocity, slope_y):
    degrees = coef.shape[1]
    rows, gx_size = slope_y.shape[1:]
    kz_size, kx_size, gz_size = degrees * narrow, LANES * wide, rows * wide
    pairs = wide // 2
    values, slopes = z_tables(gz_size, kz_size)
    basis = x_table(gx_size, kx_size)
    zt = np.concatenate(
        [values.reshape(wide, rows, kz_size), slopes.reshape(wide, rows, kz_size)], axis=1
    )
    bt = np.ascontiguousarray(basis.T).reshape(pairs, 2 * LANES, gx_size)
    vt = np.ascontiguousarray(values.T).reshape(narrow, degrees, gz_size)
    hbm = pl.BlockSpec(memory_space=pltpu.HBM)
    dma = pltpu.SemaphoreType.DMA
    return pl.pallas_call(
        functools.partial(kernel, wide, narrow, rows, gx_size),
        out_shape=(
            jax.ShapeDtypeStruct(coef.shape, BF16),
            jax.ShapeDtypeStruct(slope_y.shape, BF16),
        ),
        in_specs=[hbm] * 6,
        out_specs=(hbm, hbm),
        scratch_shapes=[
            pltpu.VMEM(zt.shape, BF16),
            pltpu.VMEM(bt.shape, BF16),
            pltpu.VMEM(vt.shape, BF16),
            pltpu.VMEM(velocity.shape, BF16),
            pltpu.VMEM(slope_y.shape, BF16),
            pltpu.VMEM((narrow, degrees, LANES), BF16),
            pltpu.VMEM((wide, 2 * rows, LANES), BF16),
            pltpu.VMEM((wide, 2 * rows, LANES), BF16),
            pltpu.VMEM((3 * rows, gx_size), F32),
            pltpu.VMEM((rows, gx_size), BF16),
            pltpu.VMEM(slope_y.shape, BF16),
            pltpu.VMEM((wide, rows, LANES), BF16),
            pltpu.VMEM((wide, rows, LANES), BF16),
            pltpu.VMEM((narrow, degrees, LANES), BF16),
            dma((8,)),
            dma((narrow,)),
            dma((narrow,)),
            dma((wide,)),
            dma((wide,)),
            dma((wide,)),
            dma((wide,)),
            dma((narrow,)),
            dma((narrow,)),
        ],
        compiler_params=pltpu.CompilerParams(
            collective_id=0, has_side_effects=True, vmem_limit_bytes=VMEM_BYTES
        ),
    )(coef, velocity, slope_y, zt, bt, vt)


def x_slope(wave_in, gx_size):
    width_now = wave_in.shape[-1]
    paired = wave_in.astype(F32).reshape(wave_in.shape[:-1] + (width_now // 2, 2))
    harmonic = lax.iota(jnp.int32, width_now // 2).astype(F32)
    omega_rate = harmonic * (2.0 * math.pi / gx_size)
    cos_part = omega_rate * paired[..., 1]
    sin_part = -omega_rate * paired[..., 0]
    return jnp.stack([cos_part, sin_part], axis=-1).reshape(wave_in.shape).astype(BF16)


def by_collectives(wide, narrow, coef, velocity, slope_y):
    gz_size, gx_size = slope_y.shape[1] * wide, slope_y.shape[2]
    kz_size, kx_size = coef.shape[1] * narrow, coef.shape[2] * wide
    values, slopes = z_tables(gz_size, kz_size)
    basis = x_table(gx_size, kx_size)
    einsum = functools.partial(jnp.einsum, preferred_element_type=F32)
    swap = functools.partial(lax.all_to_all, tiled=True)
    plane = swap(coef, "narrow", split_axis=0, concat_axis=1)
    wave_val = einsum("jn,ynk->yjk", values, plane).astype(BF16)
    wave_dz = einsum("jn,ynk->yjk", slopes, plane).astype(BF16)
    wave_val = swap(wave_val, "wide", split_axis=1, concat_axis=2)
    wave_dz = swap(wave_dz, "wide", split_axis=1, concat_axis=2)
    grid_val, grid_dx, grid_dz = (
        einsum("yjk,gk->yjg", field, basis)
        for field in (wave_val, x_slope(wave_val, gx_size), wave_dz)
    )
    total = velocity[0] * grid_dx + velocity[1] * slope_y.astype(F32) + velocity[2] * grid_dz
    half_coef = einsum("yjg,gk->yjk", (-total).astype(BF16), basis).astype(BF16)
    half_coef = swap(half_coef, "wide", split_axis=2, concat_axis=1)
    coef_z = einsum("jn,yjk->ynk", values, half_coef).astype(BF16)
    advect = swap(coef_z, "narrow", split_axis=1, concat_axis=0)
    return advect, grid_val.astype(BF16)


def solution(mesh):
    wide, narrow = mesh.shape["wide"], mesh.shape["narrow"]

    def on_device(coef, velocity, slope_y):
        whole_tiles = (
            slope_y.shape[0] == 1
            and coef.shape[1] % 16 == 0
            and coef.shape[2] == LANES
            and slope_y.shape[1] % 16 == 0
            and slope_y.shape[2] % 512 == 0
            and wide >= 4
            and wide & (wide - 1) == 0
        )
        plan = by_kernel if whole_tiles else by_collectives
        return plan(wide, narrow, coef, velocity, slope_y)

    return jax.shard_map(
        on_device,
        mesh=mesh,
        in_specs=(
            P(None, "narrow", "wide"),
            P(None, "narrow", "wide", None),
            P("narrow", "wide", None),
        ),
        out_specs=(P(None, "narrow", "wide"), P("narrow", "wide", None)),
        check_vma=False,
    )
```

```python
import functools
import math

import jax
import jax.numpy as jnp
import ml_dtypes
import numpy as np
from jax import lax
from jax.experimental import pallas as pl
from jax.experimental.pallas import tpu as pltpu
from jax.sharding import PartitionSpec as P

MESH = pl.DeviceIdType.MESH
F32 = jnp.float32
BF16 = jnp.bfloat16
LANES = 128
VMEM_BYTES = 64 * 1024 * 1024 - 256 * 1024


def x_table(gx_size, kx_size):
    points = np.arange(gx_size, dtype=np.int32)[:, None]
    column_id = np.arange(kx_size, dtype=np.int32)[None, :]
    harmonic = column_id // 2
    angles = (harmonic * points % gx_size).astype(np.float32) * np.float32(2.0 * math.pi / gx_size)
    weights = np.where(
        harmonic == 0, math.sqrt(1.0 / gx_size), math.sqrt(2.0 / gx_size)
    ).astype(np.float32)
    raw = np.where(column_id % 2 == 0, np.cos(angles), np.sin(angles))
    return (raw * weights).astype(ml_dtypes.bfloat16)


def z_tables(gz_size, kz_size):
    nodes = np.arange(gz_size, dtype=np.int32)[:, None]
    degree = np.arange(kz_size, dtype=np.int32)[None, :]
    step = np.float32(math.pi / (2.0 * gz_size))
    angles = (degree * (2 * nodes + 1) % (4 * gz_size)).astype(np.float32) * step
    polar = (2 * nodes + 1).astype(np.float32) * step
    weights = np.where(
        degree == 0, math.sqrt(1.0 / gz_size), math.sqrt(2.0 / gz_size)
    ).astype(np.float32)
    values = weights * np.cos(angles)
    slopes = weights * np.float32(2.0 / gz_size) * degree.astype(np.float32)
    slopes = slopes * np.sin(angles) / np.sin(polar)
    return values.astype(ml_dtypes.bfloat16), slopes.astype(ml_dtypes.bfloat16)


def dot(left, right):
    return jnp.dot(left, right, preferred_element_type=F32)


def dot_last(left, right):
    return lax.dot_general(left, right, (((1,), (1,)), ((), ())), preferred_element_type=F32)


def flip_bits(index, mask, size):
    total, bit = 0, 1
    while bit < size:
        digit = lax.rem(lax.div(index, bit), 2)
        total = total + bit * (1 - digit if mask & bit else digit)
        bit *= 2
    return total


def kernel(
    wide, narrow, rows, gx_size,
    coef, velocity, slope_y, zt_hbm, bt_hbm, vt_hbm,
    advect_out, grid_out,
    zt, bt, vt, speed, dy,
    recv_a, send_b, recv_b, acc, adv, buoy, send_e, recv_e, send_f,
    local_sem, a_send, a_recv, b_send, b_recv, e_send, e_recv, f_send, f_recv,
):
    pairs = wide // 2
    w = lax.axis_index("wide")
    m = lax.axis_index("narrow")
    mine = lax.div(w, 2)
    beside = 2 * mine + 1 - lax.rem(w, 2)
    narrow_peers = [lax.rem(m + r, narrow) for r in range(1, narrow)]
    pair_of = [flip_bits(mine, t, pairs) for t in range(pairs)]
    far_first = list(range(pairs - 1, 0, -1))

    own = pltpu.make_async_copy(coef.at[m], recv_a.at[m], local_sem.at[0])
    own.start()
    loads = [
        pltpu.make_async_copy(src, dst, local_sem.at[1 + i])
        for i, (src, dst) in enumerate(
            [(zt_hbm, zt), (bt_hbm, bt), (velocity, speed), (slope_y, dy), (vt_hbm, vt)]
        )
    ]
    for load in loads[:2]:
        load.start()

    barrier = pltpu.get_barrier_semaphore()
    for peer in narrow_peers:
        pl.semaphore_signal(barrier, inc=1, device_id={"narrow": peer}, device_id_type=MESH)
    for t in range(1, wide):
        pl.semaphore_signal(
            barrier, inc=1, device_id={"wide": lax.rem(w + t, wide)}, device_id_type=MESH
        )
    pl.semaphore_wait(barrier, narrow + wide - 2)

    sends = []

    def push(src, dst, send_sem, recv_sem, target):
        copy = pltpu.make_async_remote_copy(
            src_ref=src, dst_ref=dst, send_sem=send_sem, recv_sem=recv_sem,
            device_id=target, device_id_type=MESH,
        )
        copy.start()
        sends.append(copy)

    def arrived(dst, recv_sem, send_sem, target):
        pltpu.make_async_remote_copy(
            src_ref=dst, dst_ref=dst, send_sem=send_sem, recv_sem=recv_sem,
            device_id=target, device_id_type=MESH,
        ).wait_recv()

    for peer in narrow_peers:
        push(coef.at[peer], recv_a.at[m], a_send.at[peer], a_recv.at[m], {"narrow": peer})
    own.wait()
    loads[0].wait()
    for peer in narrow_peers:
        arrived(recv_a.at[peer], a_recv.at[peer], a_send.at[peer], {"narrow": peer})

    plane = recv_a[...].reshape(-1, LANES)

    for t in far_first + [0]:
        both = pl.ds(2 * pair_of[t], 2)
        fields = dot(zt[both].reshape(4 * rows, -1), plane).astype(BF16)
        send_b[both] = fields.reshape(2, 2 * rows, LANES)
        for d in (2 * pair_of[t], 2 * pair_of[t] + 1) if t else (beside,):
            push(send_b.at[d], recv_b.at[w], b_send.at[d], b_recv.at[w], {"wide": d})
    recv_b[w] = send_b[w]
    for load in loads[2:]:
        load.start()
    recv_b[w] = dot(zt[w], plane).astype(BF16)

    lane = lax.broadcasted_iota(jnp.int32, (1, LANES), 1)
    even = lax.rem(lane, 2) == 0

    def slope_of(field, first):
        harmonic = (lax.div(lane, 2) + first).astype(F32)
        rate = harmonic * (2.0 * math.pi / gx_size)
        wide_field = field.astype(F32)
        after = pltpu.roll(wide_field, LANES - 1, 1)
        before = pltpu.roll(wide_field, 1, 1)
        return jnp.where(even, rate * after, -rate * before).astype(BF16)

    def stacked(pair):
        fields = []
        for s in (0, 1):
            block = recv_b[2 * pair + s]
            val, dz = block[:rows], block[rows:]
            dx = slope_of(val, (2 * pair + s) * (LANES // 2))
            fields.append(jnp.concatenate([val, dx, dz], axis=0))
        return jnp.concatenate(fields, axis=1)

    tile = 512
    cuts = [slice(c, c + tile) for c in range(0, gx_size, tile)]
    for t in range(pairs):
        pair = pair_of[t]
        if t == 0:
            arrived(recv_b.at[beside], b_recv.at[beside], b_send.at[beside], {"wide": beside})
            loads[1].wait()
        else:
            for d in (2 * pair, 2 * pair + 1):
                arrived(recv_b.at[d], b_recv.at[d], b_send.at[d], {"wide": d})
        fields = stacked(pair)
        if t == pairs - 1:
            loads[2].wait()
            loads[3].wait()
        for cut in cuts:
            part = dot(fields, bt[pair, :, cut])
            if t > 0:
                part = part + acc[:, cut]
            if t < pairs - 1:
                acc[:, cut] = part
            else:
                buoy[0, :, cut] = part[:rows].astype(BF16)
                total = speed[0, 0, :, cut].astype(F32) * part[rows : 2 * rows]
                total = total + speed[1, 0, :, cut].astype(F32) * dy[0, :, cut].astype(F32)
                total = total + speed[2, 0, :, cut].astype(F32) * part[2 * rows :]
                adv[:, cut] = (-total).astype(BF16)
    grid_copy = pltpu.make_async_copy(buoy, grid_out, local_sem.at[6])
    grid_copy.start()

    for t in far_first + [0]:
        pair = pair_of[t]
        half = dot_last(adv[...], bt[pair]).astype(BF16)
        for s in (0, 1):
            send_e[2 * pair + s] = half[:, s * LANES : (s + 1) * LANES]
        for d in (2 * pair, 2 * pair + 1) if t else (beside,):
            push(send_e.at[d], recv_e.at[w], e_send.at[d], e_recv.at[w], {"wide": d})
    recv_e[w] = send_e[w]
    loads[4].wait()
    for t in range(pairs):
        for d in (2 * pair_of[t], 2 * pair_of[t] + 1) if t else (beside,):
            arrived(recv_e.at[d], e_recv.at[d], e_send.at[d], {"wide": d})

    points = recv_e[...].reshape(-1, LANES)
    for peer in narrow_peers:
        send_f[peer] = dot(vt[peer], points).astype(BF16)
        push(send_f.at[peer], advect_out.at[m], f_send.at[peer], f_recv.at[m], {"narrow": peer})
    send_f[m] = dot(vt[m], points).astype(BF16)
    kept = pltpu.make_async_copy(send_f.at[m], advect_out.at[m], local_sem.at[7])
    kept.start()
    for peer in narrow_peers:
        arrived(advect_out.at[peer], f_recv.at[peer], f_send.at[peer], {"narrow": peer})
    kept.wait()
    grid_copy.wait()
    for copy in sends:
        copy.wait_send()


def hand_over(advect, grid, advect_out, grid_out, advect_held, grid_held, sem):
    routes = [(advect, advect_held, advect_out), (grid, grid_held, grid_out)]
    fetches = [
        pltpu.make_async_copy(src, held, sem.at[i]) for i, (src, held, _) in enumerate(routes)
    ]
    stores = [
        pltpu.make_async_copy(held, dst, sem.at[2 + i]) for i, (_, held, dst) in enumerate(routes)
    ]
    for fetch in fetches:
        fetch.start()
    for fetch, store in zip(fetches, stores):
        fetch.wait()
        store.start()
    for store in stores:
        store.wait()


def by_kernel(wide, narrow, coef, velocity, slope_y):
    degrees = coef.shape[1]
    rows, gx_size = slope_y.shape[1:]
    kz_size, kx_size, gz_size = degrees * narrow, LANES * wide, rows * wide
    pairs = wide // 2
    values, slopes = z_tables(gz_size, kz_size)
    basis = x_table(gx_size, kx_size)
    zt = np.concatenate(
        [values.reshape(wide, rows, kz_size), slopes.reshape(wide, rows, kz_size)], axis=1
    )
    bt = np.ascontiguousarray(basis.T).reshape(pairs, 2 * LANES, gx_size)
    vt = np.ascontiguousarray(values.T).reshape(narrow, degrees, gz_size)
    hbm = pl.BlockSpec(memory_space=pltpu.HBM)
    dma = pltpu.SemaphoreType.DMA
    advect, grid = pl.pallas_call(
        functools.partial(kernel, wide, narrow, rows, gx_size),
        out_shape=(
            jax.ShapeDtypeStruct(coef.shape, BF16),
            jax.ShapeDtypeStruct(slope_y.shape, BF16),
        ),
        in_specs=[hbm] * 6,
        out_specs=(hbm, hbm),
        scratch_shapes=[
            pltpu.VMEM(zt.shape, BF16),
            pltpu.VMEM(bt.shape, BF16),
            pltpu.VMEM(vt.shape, BF16),
            pltpu.VMEM(velocity.shape, BF16),
            pltpu.VMEM(slope_y.shape, BF16),
            pltpu.VMEM((narrow, degrees, LANES), BF16),
            pltpu.VMEM((wide, 2 * rows, LANES), BF16),
            pltpu.VMEM((wide, 2 * rows, LANES), BF16),
            pltpu.VMEM((3 * rows, gx_size), F32),
            pltpu.VMEM((rows, gx_size), BF16),
            pltpu.VMEM(slope_y.shape, BF16),
            pltpu.VMEM((wide, rows, LANES), BF16),
            pltpu.VMEM((wide, rows, LANES), BF16),
            pltpu.VMEM((narrow, degrees, LANES), BF16),
            dma((8,)),
            dma((narrow,)),
            dma((narrow,)),
            dma((wide,)),
            dma((wide,)),
            dma((wide,)),
            dma((wide,)),
            dma((narrow,)),
            dma((narrow,)),
        ],
        compiler_params=pltpu.CompilerParams(
            collective_id=0, has_side_effects=True, vmem_limit_bytes=VMEM_BYTES
        ),
    )(coef, velocity, slope_y, zt, bt, vt)
    return pl.pallas_call(
        hand_over,
        out_shape=(
            jax.ShapeDtypeStruct(coef.shape, BF16),
            jax.ShapeDtypeStruct(slope_y.shape, BF16),
        ),
        in_specs=[hbm] * 2,
        out_specs=(hbm, hbm),
        scratch_shapes=[
            pltpu.VMEM(coef.shape, BF16),
            pltpu.VMEM(slope_y.shape, BF16),
            dma((4,)),
        ],
        compiler_params=pltpu.CompilerParams(vmem_limit_bytes=VMEM_BYTES),
    )(advect, grid)


def x_slope(wave_in, gx_size):
    width_now = wave_in.shape[-1]
    paired = wave_in.astype(F32).reshape(wave_in.shape[:-1] + (width_now // 2, 2))
    harmonic = lax.iota(jnp.int32, width_now // 2).astype(F32)
    omega_rate = harmonic * (2.0 * math.pi / gx_size)
    cos_part = omega_rate * paired[..., 1]
    sin_part = -omega_rate * paired[..., 0]
    return jnp.stack([cos_part, sin_part], axis=-1).reshape(wave_in.shape).astype(BF16)


def by_collectives(wide, narrow, coef, velocity, slope_y):
    gz_size, gx_size = slope_y.shape[1] * wide, slope_y.shape[2]
    kz_size, kx_size = coef.shape[1] * narrow, coef.shape[2] * wide
    values, slopes = z_tables(gz_size, kz_size)
    basis = x_table(gx_size, kx_size)
    einsum = functools.partial(jnp.einsum, preferred_element_type=F32)
    swap = functools.partial(lax.all_to_all, tiled=True)
    plane = swap(coef, "narrow", split_axis=0, concat_axis=1)
    wave_val = einsum("jn,ynk->yjk", values, plane).astype(BF16)
    wave_dz = einsum("jn,ynk->yjk", slopes, plane).astype(BF16)
    wave_val = swap(wave_val, "wide", split_axis=1, concat_axis=2)
    wave_dz = swap(wave_dz, "wide", split_axis=1, concat_axis=2)
    grid_val, grid_dx, grid_dz = (
        einsum("yjk,gk->yjg", field, basis)
        for field in (wave_val, x_slope(wave_val, gx_size), wave_dz)
    )
    total = velocity[0] * grid_dx + velocity[1] * slope_y.astype(F32) + velocity[2] * grid_dz
    half_coef = einsum("yjg,gk->yjk", (-total).astype(BF16), basis).astype(BF16)
    half_coef = swap(half_coef, "wide", split_axis=2, concat_axis=1)
    coef_z = einsum("jn,yjk->ynk", values, half_coef).astype(BF16)
    advect = swap(coef_z, "narrow", split_axis=1, concat_axis=0)
    return advect, grid_val.astype(BF16)


def solution(mesh):
    wide, narrow = mesh.shape["wide"], mesh.shape["narrow"]

    def on_device(coef, velocity, slope_y):
        whole_tiles = (
            slope_y.shape[0] == 1
            and coef.shape[1] % 16 == 0
            and coef.shape[2] == LANES
            and slope_y.shape[1] % 16 == 0
            and slope_y.shape[2] % 512 == 0
            and wide >= 4
            and wide & (wide - 1) == 0
        )
        plan = by_kernel if whole_tiles else by_collectives
        return plan(wide, narrow, coef, velocity, slope_y)

    return jax.shard_map(
        on_device,
        mesh=mesh,
        in_specs=(
            P(None, "narrow", "wide"),
            P(None, "narrow", "wide", None),
            P("narrow", "wide", None),
        ),
        out_specs=(P(None, "narrow", "wide"), P("narrow", "wide", None)),
        check_vma=False,
    )
```
